128 devices in a mesh: dp: 16 (over z_lo, y, core), vocab: 8 (over z_hi, x).
Axes of the slice: x: 4, y: 4, z: 4 (z_hi: 2, z_lo: 2; z = z_hi * 2 + z_lo), core: 2. Of those that a mesh axis runs over, the one named last changes fastest.
Arguments:
- hidden: bfloat16 [768, 6144], P('dp')
- targets: int32 [768], replicated, may hold values from 0 to 50431
- hidden_probe: bfloat16 [768, 6144], replicated, may hold values from -1 to 1, as said below
- table: bfloat16 [50432, 6144], P(('dp', 'vocab')), as said below
- table_probe: bfloat16 [50432, 6144], P(('dp', 'vocab')), may hold values from -1 to 1, as said below
Outputs:
- hidden_tangent: bfloat16 [768, 6144], P('dp', 'vocab')
- curvature: float32 [50432], P(('dp', 'vocab'))
The draws below stay inside these ranges and needn't reach their ends.
Inputs may be any that keep to these rules, and one draw needn't show every extreme that they name: `hidden_probe`: entries are +1 or -1. `table`: rows of the output head. `table_probe`: entries are +1 or -1.
All inputs are finite; a program needn't handle non-finite values.
Results may differ from the reference program's by a relative error of at most 0.004.
Values may be sent and summed in bfloat16 or wider, within the bound.
No kernel may reach another device: no remote copies, remote signals or barrier semaphores. Data moves between devices by JAX's collectives and lax.ppermute only.
A program may use at most 128 MiB of HBM per device.

```python
import math
import jax
import jax.numpy as jnp
from jax import lax

D = 6144
V = 50432
TOKENS = 768


def base_table(key):
    return jnp.clip(jax.random.normal(jax.random.fold_in(key, 101), (V, D), jnp.float32), -5.0, 5.0)


def drawn_rows(key):
    return jax.random.permutation(jax.random.fold_in(key, 202), V // 2)[:8]


def strength_list():
    return jnp.array([0.5, 0.75, 1.0, 1.25, 1.5, 0.5, 1.0, 1.5], jnp.float32)


def draw_table(key, part):
    values = base_table(key)
    chosen_rows = drawn_rows(key)
    factors = 1.0 - 2.0 / (strength_list() * 150.0)
    values = values.at[chosen_rows + V // 2].set(values[chosen_rows] * factors[:, None])
    return (values * (3.0 / math.sqrt(D))).astype(jnp.bfloat16)


def draw_hidden(key, part):
    base_key = key
    key = jax.random.fold_in(key, 3)
    values = jnp.clip(jax.random.normal(key, (TOKENS, D), jnp.float32), -5.0, 5.0)
    chosen_rows = drawn_rows(base_key)
    chosen_tokens = jax.random.permutation(jax.random.fold_in(key, 5), TOKENS)[:8]
    amplitude = strength_list() * (50.0 / math.sqrt(D))
    values = values.at[chosen_tokens].set(base_table(base_key)[chosen_rows] * amplitude[:, None])
    return values.astype(jnp.bfloat16)


def draw_hidden_probe(key, part):
    key = jax.random.fold_in(key, 7)
    return jnp.where(jax.random.bernoulli(key, 0.5, (TOKENS, D)), 1.0, -1.0).astype(jnp.bfloat16)


def draw_table_probe(key, part):
    key = jax.random.fold_in(key, 9)
    return jnp.where(jax.random.bernoulli(key, 0.5, (V, D)), 1.0, -1.0).astype(jnp.bfloat16)


def plant(entries, key, low, largest):
    place = [jax.random.randint(jax.random.fold_in(key, axis), (), 0, length) for axis, length in enumerate(entries.shape)]
    widest = entries.shape.index(max(entries.shape))
    neighbour = place[:widest] + [(place[widest] + 1) % entries.shape[widest]] + place[widest + 1:]
    return entries.at[tuple(place)].set(low).at[tuple(neighbour)].set(largest)


def setup_inputs(seed: int = 0) -> dict:
    streams_of = jax.random.split(jax.random.key(seed), 6)
    return {
        "hidden": draw_hidden(jax.random.fold_in(streams_of[5], 71), 0),
        "targets": plant(jax.random.randint(streams_of[1], (TOKENS,), 0, V), jax.random.fold_in(streams_of[1], 1), 0, V - 1).astype(jnp.int32),
        "hidden_probe": draw_hidden_probe(jax.random.fold_in(streams_of[5], 71), 0),
        "table": draw_table(jax.random.fold_in(streams_of[5], 71), 0),
        "table_probe": draw_table_probe(jax.random.fold_in(streams_of[5], 71), 0),
    }


CONTRACT = (((1,), (1,)), ((), ()))

def row_products(matrix, weights):
    return lax.dot_general(matrix, weights, CONTRACT, preferred_element_type=jnp.float32)

def reference(hidden, targets, hidden_probe, table, table_probe):
    probe_scale = 1.0 / math.sqrt(D)
    logits = row_products(hidden, table)
    hidden_side = row_products(hidden, table_probe) * probe_scale
    tangent = row_products(hidden_probe, table) + hidden_side
    probe_side = row_products(hidden_probe, table_probe) * probe_scale
    highest = lax.optimization_barrier(jnp.max(logits, axis=1, keepdims=True))
    weights_exp = jnp.exp(logits - highest)
    normal_sum = lax.optimization_barrier(jnp.sum(weights_exp, axis=1, keepdims=True))
    weighted_sum = lax.optimization_barrier(jnp.sum(weights_exp * tangent, axis=1, keepdims=True))
    probability = weights_exp / normal_sum
    mean_tangent = weighted_sum / normal_sum
    curve_term = probability * (tangent - mean_tangent)
    columns = jnp.arange(V, dtype=jnp.int32)[None, :]
    onehot = (targets[:, None] == columns).astype(jnp.float32)
    gradient = probability - onehot
    curve_half = curve_term.astype(jnp.bfloat16)
    gradient_half = gradient.astype(jnp.bfloat16)
    summed = math.sqrt(D) * jnp.dot(curve_half, table, preferred_element_type=jnp.float32)
    summed = summed + jnp.dot(gradient_half, table_probe, preferred_element_type=jnp.float32)
    hidden_tangent = summed.astype(jnp.bfloat16)
    curvature = lax.optimization_barrier(jnp.sum(curve_term * hidden_side + gradient * probe_side, axis=0)) * (V / TOKENS)
    return (hidden_tangent, curvature)
```

```python
import math

import jax
import jax.numpy as jnp
from jax import lax
from jax.experimental import pallas as pl
from jax.experimental.pallas import tpu as pltpu
from jax.sharding import PartitionSpec as P

AXES = ("dp", "vocab")
F32 = jnp.float32
BF16 = jnp.bfloat16
FIRST = 3072
BLOCK = 1024
ROWS = 48
MIB = 1 << 20
NT = (((1,), (1,)), ((), ()))


def decode(d):
    return (d >> 6) & 1, (d >> 4) & 3, (d >> 3) & 1, (d >> 2) & 1, d & 3


def encode(zl, y, c, zh, x):
    return (((zl * 4 + y) * 2 + c) * 2 + zh) * 4 + x


def pairs(axes, kind):
    out = []
    for d in range(128):
        zl, y, c, zh, x = decode(d)
        m = 1 if c == kind else 3
        for axis in axes:
            if axis == "x":
                x ^= m
            elif axis == "y":
                y ^= m
            elif axis == "z":
                z = (2 * zh + zl) ^ m
                zh, zl = z >> 1, z & 1
            else:
                c ^= 1
        out.append((d, encode(zl, y, c, zh, x)))
    return out


def swap(a, axis, kind=0):
    return lax.ppermute(a, AXES, pairs(axis, kind))


def pair_of(c, q):
    return jnp.where(c == 0, (q ^ (q >> 1)) & 1, q >> 1)


def bit_of(c, q):
    return jnp.where(c == 0, q >> 1, q & 1)


def member(c, pair, bit):
    return jnp.where(c == 0, pair * (1 + bit) + (1 - pair) * 3 * bit, 2 * pair + bit)


def slot_of(c, me, q):
    return 2 * (pair_of(c, me) ^ pair_of(c, q)) + bit_of(c, q)


def groups_of_eight():
    found = {}
    for d in range(128):
        zl, y, c, zh, x = decode(d)
        at = [2 * zh + zl, y, x]
        pair = [(q ^ (q >> 1)) & 1 if c == 0 else q >> 1 for q in at]
        bit = [q >> 1 if c == 0 else q & 1 for q in at]
        found.setdefault((c, *pair), {})[tuple(bit)] = d
    return [[g[b] for b in sorted(g)] for g in found.values()]


def groups_of_core():
    return [[d for d in range(128) if decode(d)[2] == c] for c in range(2)]


def row_place(me, slot):
    zl, y, c, _, _ = decode(me)
    zs, ys = slot // 4, slot % 4
    return (zl ^ zs) * 4 + (y ^ jnp.where(c == 0, (0, 3, 1, 2)[ys], (0, 1, 3, 2)[ys]))


def owner(me, slot):
    return row_place(me, slot) * 2 + ((me >> 3) & 1)


def tie(array, *after):
    def kernel(*refs):
        del refs

    return pl.pallas_call(
        kernel,
        in_specs=[pl.BlockSpec(memory_space=pl.ANY)] * (1 + len(after)),
        out_specs=pl.BlockSpec(memory_space=pl.ANY),
        out_shape=jax.ShapeDtypeStruct(array.shape, array.dtype),
        input_output_aliases={0: 0},
    )(array, *after)


def doubled(held, axis, kind=0):
    return jnp.concatenate([held, swap(held, axis, kind)], axis=0 if axis == "z" else 1)


def products(me, rows, tables, start, before=(), tangents=(), scale=1.0, after=()):
    picked = rows.ndim == 3
    m, k = 8 * ROWS, rows.shape[-1]
    n = tables[0].shape[0]
    count = len(tables)
    steps = k // BLOCK
    first = start // BLOCK
    row_specs = (
        [pl.BlockSpec((1, ROWS, BLOCK), lambda s, me, i=i: (owner(me[0], i), 0, s)) for i in range(8)]
        if picked
        else [pl.BlockSpec((m, BLOCK), lambda s, me: (0, s))]
    )

    def kernel(me_ref, *refs):
        refs = list(refs)

        def take(length):
            taken = refs[:length]
            del refs[:length]
            return taken

        row_refs = take(len(row_specs))
        table_refs = take(count)
        prior_refs = take(len(before))
        extra_refs = take(len(tangents))
        take(len(after))
        outs = take(count)
        step = pl.program_id(0)
        if picked:
            block = jnp.concatenate([r[0] for r in row_refs], axis=0)
        else:
            block = row_refs[0][...]

        @pl.when(step == 0)
        def _():
            for i in range(count):
                outs[i][...] = prior_refs[i][...] if before else jnp.zeros((m, n), F32)

        for i in range(count):
            outs[i][...] += lax.dot_general(block, table_refs[i][...], NT, preferred_element_type=F32)

        if tangents:
            stats_ref, packed_ref = take(2)

            @pl.when(step == steps - 1)
            def _():
                lane = lax.broadcasted_iota(jnp.int32, (ROWS, 128), 1)
                for i in range(8):
                    at = slice(i * ROWS, (i + 1) * ROWS)
                    l0, l1 = outs[0][at, :], outs[1][at, :]
                    t0 = extra_refs[0][at, :] + outs[2][at, :] * scale
                    t1 = extra_refs[1][at, :] + outs[3][at, :] * scale
                    top = jnp.maximum(
                        jnp.max(l0, axis=1, keepdims=True), jnp.max(l1, axis=1, keepdims=True)
                    )
                    e0 = jnp.exp(l0 - top)
                    e1 = jnp.exp(l1 - top)
                    total = jnp.sum(e0, axis=1, keepdims=True) + jnp.sum(e1, axis=1, keepdims=True)
                    weighted = jnp.sum(e0 * t0, axis=1, keepdims=True) + jnp.sum(
                        e1 * t1, axis=1, keepdims=True
                    )
                    place = pl.multiple_of(row_place(me_ref[0], i) * ROWS, ROWS)
                    packed_ref[pl.ds(place, ROWS), :] = jnp.where(
                        lane == 0, top, jnp.where(lane == 1, total, weighted)
                    )
                stats_ref[...] = packed_ref[...].T[0:3, :]

    whole = pl.BlockSpec((m, n), lambda s, me: (0, 0))
    out_shape = [jax.ShapeDtypeStruct((m, n), F32)] * count
    out_specs = [whole] * count
    scratch = []
    if tangents:
        out_shape.append(jax.ShapeDtypeStruct((3, m), F32))
        out_specs.append(pl.BlockSpec((3, m), lambda s, me: (0, 0)))
        scratch.append(pltpu.VMEM((m, 128), F32))
    inputs = [me, *([rows] * len(row_specs)), *tables, *before, *tangents, *after]
    return pl.pallas_call(
        kernel,
        grid_spec=pltpu.PrefetchScalarGridSpec(
            num_scalar_prefetch=1,
            grid=(steps,),
            in_specs=row_specs
            + [pl.BlockSpec((n, BLOCK), lambda s, me: (0, s + first))] * count
            + [whole] * (len(before) + len(tangents))
            + [pl.BlockSpec(memory_space=pl.ANY)] * len(after),
            out_specs=out_specs,
            scratch_shapes=scratch,
        ),
        out_shape=out_shape,
        compiler_params=pltpu.CompilerParams(vmem_limit_bytes=40 * MIB),
        cost_estimate=pl.CostEstimate(
            flops=MIB, bytes_accessed=MIB, transcendentals=0
        ),
    )(*inputs)


def coefficients(me, logits, sides, tangents, probes, stats, targets, scale):
    m, n = logits[0].shape

    def kernel(me_ref, *refs):
        l_refs, h_refs, t_refs, p_refs = refs[0:2], refs[2:4], refs[4:6], refs[6:8]
        stats_ref, targets_ref = refs[8:10]
        c_refs, g_refs, curve_ref, column_ref = refs[10:12], refs[12:14], refs[14], refs[15]
        here = me_ref[0]
        tops = stats_ref[:, 0, :]
        top = jnp.max(tops, axis=0, keepdims=True)
        factor = jnp.exp(tops - top)
        total = jnp.sum(stats_ref[:, 1, :] * factor, axis=0, keepdims=True)
        mean = jnp.sum(stats_ref[:, 2, :] * factor, axis=0, keepdims=True) / total
        inverse = 1.0 / total
        line = lax.broadcasted_iota(jnp.int32, (128, m), 0)
        column_ref[...] = jnp.where(line == 0, top, jnp.where(line == 1, inverse, mean)).T
        for i in range(2):
            vocab_start = (here ^ (8 * i)) * n
            curve_sum = jnp.zeros((1, n), F32)
            for j in range(8):
                at = slice(j * ROWS, (j + 1) * ROWS)
                place = row_place(here, j)
                values = column_ref[pl.ds(pl.multiple_of(place * ROWS, ROWS), ROWS), :]
                mine = pl.multiple_of(owner(here, j) * ROWS, ROWS)
                wanted = targets_ref[pl.ds(mine, ROWS), :]
                side = h_refs[i][at, :] * scale
                tangent = t_refs[i][at, :] + side
                probability = jnp.exp(l_refs[i][at, :] - values[:, 0:1]) * values[:, 1:2]
                curve = probability * (tangent - values[:, 2:3])
                column = lax.broadcasted_iota(jnp.int32, (ROWS, n), 1) + vocab_start
                gradient = probability - jnp.where(wanted == column, 1.0, 0.0)
                c_refs[i][at, :] = curve.astype(BF16)
                g_refs[i][at, :] = gradient.astype(BF16)
                curve_sum += jnp.sum(
                    curve * side + gradient * (p_refs[i][at, :] * scale), axis=0, keepdims=True
                )
            curve_ref[i : i + 1, :] = curve_sum

    vmem = pl.BlockSpec(memory_space=pltpu.VMEM)
    return pl.pallas_call(
        kernel,
        in_specs=[pl.BlockSpec(memory_space=pltpu.SMEM)] + [vmem] * 10,
        out_specs=[vmem] * 5,
        out_shape=[jax.ShapeDtypeStruct((m, n), BF16)] * 4 + [jax.ShapeDtypeStruct((2, n), F32)],
        scratch_shapes=[pltpu.VMEM((m, 128), F32)],
        compiler_params=pltpu.CompilerParams(vmem_limit_bytes=40 * MIB),
    )(me, *logits, *sides, *tangents, *probes, stats, targets)


def back(me, curves, gradients, tables, probes, root):
    m, n = curves[0].shape
    width = 768
    part = width // 3
    kept_type = F32

    def kernel(me_ref, c0, c1, g0, g1, t0, t1, p0, p1, *outs):
        step = pl.program_id(0)
        zl, y, c, zh, _ = decode(me_ref[0])
        total = jnp.dot(c0[...], t0[...], preferred_element_type=F32)
        total += jnp.dot(c1[...], t1[...], preferred_element_type=F32)
        total *= root
        total += jnp.dot(g0[...], p0[...], preferred_element_type=F32)
        total += jnp.dot(g1[...], p1[...], preferred_element_type=F32)
        def places(slot):
            place = row_place(me_ref[0], slot)
            zs = slot_of(c, 2 * zh + zl, 2 * (zh ^ (step & 1)) + (place >> 2))
            return zs, slot_of(c, y, place & 3), slice(slot * ROWS, (slot + 1) * ROWS)

        for slot in range(8):
            zs, ys, at = places(slot)
            if slot % 4 < 2:
                outs[3][zs, ys, 0] = total[at, part : 2 * part]
            else:
                outs[2][zs, ys - 2, 0] = total[at, part : 2 * part].astype(BF16)

        @pl.when(step < 4)
        def _():
            for slot in range(8):
                zs, ys, at = places(slot)
                outs[0][zs, ys, 0] = total[at, :part].astype(BF16)

        @pl.when(step >= 4)
        def _():
            for slot in range(8):
                zs, ys, at = places(slot)
                outs[1][zs, ys, 0] = total[at, :part]

        for half_rows in range(2):
            z_slot = places(4 * half_rows)[0]

            @pl.when(z_slot >= 2)
            def _():
                for slot in range(4 * half_rows, 4 * half_rows + 4):
                    zs, ys, at = places(slot)
                    outs[4][zs - 2, ys, 0] = total[at, 2 * part :].astype(BF16)

            @pl.when(z_slot < 2)
            def _():
                for slot in range(4 * half_rows, 4 * half_rows + 4):
                    zs, ys, at = places(slot)
                    outs[5][zs, ys, 0] = total[at, 2 * part :]

    def columns(s, me):
        _, _, c, zh, x = decode(me[0])
        slot = ((s >> 1) + 2) & 3
        return (0, (zh ^ (s & 1)) * 4 + member(c, pair_of(c, x) ^ (slot >> 1), slot & 1))

    left = pl.BlockSpec((m, n), lambda s, me: (0, 0))
    right = pl.BlockSpec((n, width), columns)
    shapes, specs = [], []
    for axis in range(3):
        half = [[4, 4, 2], [4, 2, 4], [2, 4, 4]][axis]
        for kept in range(2):
            shapes.append(jax.ShapeDtypeStruct((*half, ROWS, part), kept_type if kept else BF16))

            def out_block(s, me, axis=axis, kept=kept):
                turn = s >> 1
                if axis > 0:
                    x_slot = (turn + 2) & 3
                elif kept:
                    x_slot = jnp.maximum(turn - 2, 0)
                else:
                    x_slot = jnp.minimum(turn, 1)
                return (0, 0, x_slot, 0, 0)

            specs.append(pl.BlockSpec((half[0], half[1], 1, ROWS, part), out_block))
    return pl.pallas_call(
        kernel,
        grid_spec=pltpu.PrefetchScalarGridSpec(
            num_scalar_prefetch=1,
            grid=(8,),
            in_specs=[left] * 4 + [right] * 4,
            out_specs=specs,
        ),
        out_shape=shapes,
        compiler_params=pltpu.CompilerParams(vmem_limit_bytes=40 * MIB),
        cost_estimate=pl.CostEstimate(
            flops=MIB, bytes_accessed=MIB, transcendentals=0
        ),
    )(me, *curves, *gradients, *tables, *probes)


def body(hidden, targets, hidden_probe, table, table_probe):
    vocab_rows, width = table.shape
    token_count = targets.shape[0]
    vocab_total = vocab_rows * 128
    scale = 1.0 / math.sqrt(width)
    root = math.sqrt(width)
    me = lax.axis_index(AXES).astype(jnp.int32).reshape(1)

    first = hidden[:, :FIRST].reshape(1, 1, ROWS, FIRST)
    second = hidden[:, FIRST:].reshape(1, 1, ROWS, width - FIRST)
    probe_rows = hidden_probe.reshape(token_count // ROWS, ROWS, width)
    first = doubled(first, "y", 1)
    second = doubled(second, "z")
    table_other = swap(table, "c")
    probe_other = swap(table_probe, "c")
    t0, p0 = products(me, probe_rows, (table, table_probe), 0, after=(first,))
    first = doubled(first, "y", 0)
    second = doubled(tie(second, first, t0), "y", 1)
    (t1,) = products(me, probe_rows, (table_other,), 0, after=(first,))
    first = doubled(first, "z").reshape(8 * ROWS, FIRST)
    second = doubled(tie(second, t1), "y", 0).reshape(8 * ROWS, width - FIRST)
    (p1,) = products(me, probe_rows, (probe_other,), 0)
    all_tables = (table, table_other, table_probe, probe_other)
    early = products(me, first, all_tables, 0)
    l0, l1, h0, h1, stats = products(
        me, second, all_tables, FIRST, before=early, tangents=(t0, t1), scale=scale
    )
    stats = lax.all_to_all(
        jnp.broadcast_to(stats[None], (64, *stats.shape)),
        AXES,
        0,
        0,
        axis_index_groups=groups_of_core(),
        tiled=True,
    )
    c0, c1, g0, g1, curve = coefficients(
        me, (l0, l1), (h0, h1), (t0, t1), (p0, p1), stats, targets.reshape(token_count, 1), scale
    )
    curvature = (curve[0] + swap(curve[1], "c")) * (vocab_total / token_count)

    axis_of = {"z": 0, "y": 1, "x": 2}
    summed = []
    halves = back(me, (c0, c1), (g0, g1), (table, table_other), (table_probe, probe_other), root)
    for part, axes in enumerate(("xyz", "yzx", "zxy")):
        send, keep = halves[2 * part], halves[2 * part + 1]
        for i, axis in enumerate(axes):
            keep = keep + swap(send, axis, 0).astype(F32)
            if i < 2:
                k = axis_of[axes[i + 1]]
                send = lax.slice_in_dim(keep, 2, 4, axis=k).astype(BF16)
                keep = lax.slice_in_dim(keep, 0, 2, axis=k)
        summed.append(keep)
    total = jnp.concatenate(summed, axis=-1).astype(BF16).reshape(8, ROWS, width // 8)
    total = lax.all_to_all(total, AXES, 0, 0, axis_index_groups=groups_of_eight(), tiled=True)
    return jnp.sum(total.astype(F32), axis=0).astype(BF16), curvature


def solution(mesh):
    placed = (P("dp", None), P(), P(), P(("dp", "vocab"), None), P(("dp", "vocab"), None))
    return jax.shard_map(
        body,
        mesh=mesh,
        in_specs=placed,
        out_specs=(P("dp", "vocab"), P(("dp", "vocab"))),
        check_vma=False,
    )
```

```python
import math

import jax
import jax.numpy as jnp
from jax import lax
from jax.experimental import pallas as pl
from jax.experimental.pallas import tpu as pltpu
from jax.sharding import PartitionSpec as P

AXES = ("dp", "vocab")
F32 = jnp.float32
BF16 = jnp.bfloat16
FIRST = 3072
BLOCK = 1024
PROBE_BLOCK = 2048
ROWS = 48
MIB = 1 << 20
NT = (((1,), (1,)), ((), ()))


def decode(d):
    return (d >> 6) & 1, (d >> 4) & 3, (d >> 3) & 1, (d >> 2) & 1, d & 3


def encode(zl, y, c, zh, x):
    return (((zl * 4 + y) * 2 + c) * 2 + zh) * 4 + x


def pairs(axes, kind):
    out = []
    for d in range(128):
        zl, y, c, zh, x = decode(d)
        m = 1 if c == kind else 3
        for axis in axes:
            if axis == "x":
                x ^= m
            elif axis == "y":
                y ^= m
            elif axis == "z":
                z = (2 * zh + zl) ^ m
                zh, zl = z >> 1, z & 1
            else:
                c ^= 1
        out.append((d, encode(zl, y, c, zh, x)))
    return out


def swap(a, axis, kind=0):
    return lax.ppermute(a, AXES, pairs(axis, kind))


def pair_of(c, q):
    return jnp.where(c == 0, (q ^ (q >> 1)) & 1, q >> 1)


def bit_of(c, q):
    return jnp.where(c == 0, q >> 1, q & 1)


def member(c, pair, bit):
    return jnp.where(c == 0, pair * (1 + bit) + (1 - pair) * 3 * bit, 2 * pair + bit)


def slot_of(c, me, q):
    return 2 * (pair_of(c, me) ^ pair_of(c, q)) + bit_of(c, q)


def groups_of_eight():
    found = {}
    for d in range(128):
        zl, y, c, zh, x = decode(d)
        at = [2 * zh + zl, y, x]
        pair = [(q ^ (q >> 1)) & 1 if c == 0 else q >> 1 for q in at]
        bit = [q >> 1 if c == 0 else q & 1 for q in at]
        found.setdefault((c, *pair), {})[tuple(bit)] = d
    return [[g[b] for b in sorted(g)] for g in found.values()]


def groups_of_core():
    return [[d for d in range(128) if decode(d)[2] == c] for c in range(2)]


def row_place(me, slot):
    zl, y, c, _, _ = decode(me)
    zs, ys = slot // 4, slot % 4
    return (zl ^ zs) * 4 + (y ^ jnp.where(c == 0, (0, 3, 1, 2)[ys], (0, 1, 3, 2)[ys]))


def owner(me, slot):
    return row_place(me, slot) * 2 + ((me >> 3) & 1)


def tie(array, *after):
    def kernel(*refs):
        del refs

    return pl.pallas_call(
        kernel,
        in_specs=[pl.BlockSpec(memory_space=pl.ANY)] * (1 + len(after)),
        out_specs=pl.BlockSpec(memory_space=pl.ANY),
        out_shape=jax.ShapeDtypeStruct(array.shape, array.dtype),
        input_output_aliases={0: 0},
    )(array, *after)


def probe_products(me, rows, table, after=()):
    m, k = 8 * ROWS, rows.shape[-1]
    n = table.shape[0]

    def kernel(me_ref, *refs):
        row_refs, table_ref, out_ref = refs[:8], refs[8], refs[-1]
        block = jnp.concatenate([r[0] for r in row_refs], axis=0)

        @pl.when(pl.program_id(0) == 0)
        def _():
            out_ref[...] = jnp.zeros((m, n), F32)

        out_ref[...] += lax.dot_general(block, table_ref[...], NT, preferred_element_type=F32)

    return pl.pallas_call(
        kernel,
        grid_spec=pltpu.PrefetchScalarGridSpec(
            num_scalar_prefetch=1,
            grid=(k // PROBE_BLOCK,),
            in_specs=[
                pl.BlockSpec((1, ROWS, PROBE_BLOCK), lambda s, me, i=i: (owner(me[0], i), 0, s)) for i in range(8)
            ]
            + [pl.BlockSpec((n, PROBE_BLOCK), lambda s, me: (0, s))]
            + [pl.BlockSpec(memory_space=pl.ANY)] * len(after),
            out_specs=pl.BlockSpec((m, n), lambda s, me: (0, 0)),
        ),
        out_shape=jax.ShapeDtypeStruct((m, n), F32),
        compiler_params=pltpu.CompilerParams(vmem_limit_bytes=60 * MIB),
        cost_estimate=pl.CostEstimate(flops=MIB, bytes_accessed=MIB, transcendentals=0),
    )(me, *([rows] * 8), table, *after)


def hidden_products(me, pieces, tables, tangents, scale):
    m = 8 * ROWS
    k = pieces[0].shape[1] + pieces[2].shape[1]
    n = tables[0].shape[0]
    steps = k // BLOCK
    split = FIRST // BLOCK
    pair = 2 * ROWS

    def kernel(me_ref, *refs):
        piece_refs, table_refs, tangent_refs = refs[0:4], refs[4:8], refs[8:10]
        outs, stats_ref = refs[10:14], refs[14]
        rows_ref, tables_ref, packed_ref, held_ref, sems, row_sems, table_sems = refs[15:22]
        step = pl.program_id(0)
        copies = [pltpu.make_async_copy(tangent_refs[i], held_ref.at[i], sems.at[i]) for i in range(2)]

        def row_copies(at):
            if at < split:
                parts = [(0, 0, 0, m // 2), (1, 0, m // 2, m // 2)]
                column = at * BLOCK
            else:
                parts = [(2 + i % 2, i // 2 * pair, i * pair, pair) for i in range(4)]
                column = (at - split) * BLOCK
            return [
                pltpu.make_async_copy(
                    piece_refs[p].at[pl.ds(source, length), pl.ds(column, BLOCK)],
                    rows_ref.at[at, pl.ds(target, length)],
                    row_sems.at[at, i],
                )
                for i, (p, source, target, length) in enumerate(parts)
            ]

        def table_copies(at):
            column = at * BLOCK
            return [
                pltpu.make_async_copy(
                    table_refs[i].at[:, pl.ds(column, BLOCK)], tables_ref.at[at, i], table_sems.at[at, i]
                )
                for i in range(4)
            ]

        @pl.when(step == 0)
        def _():
            for copy in row_copies(0) + table_copies(0):
                copy.start()
            for i in range(4):
                outs[i][...] = jnp.zeros((m, n), F32)

        for at in range(steps):

            @pl.when(step == at)
            def _():
                for copy in row_copies(at) + table_copies(at):
                    copy.wait()
                for then in ((1, 2) if at == 0 else (at + 2,)):
                    if then < steps:
                        for copy in row_copies(then) + table_copies(then):
                            copy.start()
                if at == 1:
                    for copy in copies:
                        copy.start()

        for i in range(4):
            outs[i][...] += lax.dot_general(
                rows_ref[step], tables_ref[step, i], NT, preferred_element_type=F32
            )

        @pl.when(step == steps - 1)
        def _():
            for copy in copies:
                copy.wait()
            lane = lax.broadcasted_iota(jnp.int32, (ROWS, 128), 1)
            for i in range(8):
                at = slice(i * ROWS, (i + 1) * ROWS)
                l0, l1 = outs[0][at, :], outs[1][at, :]
                t0 = held_ref[0, at, :] + outs[2][at, :] * scale
                t1 = held_ref[1, at, :] + outs[3][at, :] * scale
                top = jnp.maximum(jnp.max(l0, axis=1, keepdims=True), jnp.max(l1, axis=1, keepdims=True))
                e0 = jnp.exp(l0 - top)
                e1 = jnp.exp(l1 - top)
                total = jnp.sum(e0, axis=1, keepdims=True) + jnp.sum(e1, axis=1, keepdims=True)
                weighted = jnp.sum(e0 * t0, axis=1, keepdims=True) + jnp.sum(
                    e1 * t1, axis=1, keepdims=True
                )
                place = pl.multiple_of(row_place(me_ref[0], i) * ROWS, ROWS)
                packed_ref[pl.ds(place, ROWS), :] = jnp.where(
                    lane == 0, top, jnp.where(lane == 1, total, weighted)
                )
            stats_ref[...] = jnp.broadcast_to(packed_ref[...].T[0:3, :][None], (64, 3, m))

    return pl.pallas_call(
        kernel,
        grid_spec=pltpu.PrefetchScalarGridSpec(
            num_scalar_prefetch=1,
            grid=(steps,),
            in_specs=[pl.BlockSpec(memory_space=pl.ANY)] * 10,
            out_specs=[pl.BlockSpec((m, n), lambda s, me: (0, 0))] * 4
            + [pl.BlockSpec((64, 3, m), lambda s, me: (0, 0, 0))],
            scratch_shapes=[
                pltpu.VMEM((steps, m, BLOCK), BF16),
                pltpu.VMEM((steps, 4, n, BLOCK), BF16),
                pltpu.VMEM((m, 128), F32),
                pltpu.VMEM((2, m, n), F32),
                pltpu.SemaphoreType.DMA((2,)),
                pltpu.SemaphoreType.DMA((steps, 4)),
                pltpu.SemaphoreType.DMA((steps, 4)),
            ],
        ),
        out_shape=[jax.ShapeDtypeStruct((m, n), F32)] * 4 + [jax.ShapeDtypeStruct((64, 3, m), F32)],
        compiler_params=pltpu.CompilerParams(vmem_limit_bytes=60 * MIB),
        cost_estimate=pl.CostEstimate(flops=MIB, bytes_accessed=MIB, transcendentals=0),
    )(me, *pieces, *tables, *tangents)


def coefficients(me, logits, sides, tangents, probes, stats, targets, scale):
    m, n = logits[0].shape

    def kernel(me_ref, *refs):
        l_refs, h_refs, t_refs, p_refs = refs[0:2], refs[2:4], refs[4:6], refs[6:8]
        stats_ref, targets_ref = refs[8:10]
        c_refs, g_refs, curve_ref, column_ref = refs[10:12], refs[12:14], refs[14], refs[15]
        here = me_ref[0]
        tops = stats_ref[:, 0, :]
        top = jnp.max(tops, axis=0, keepdims=True)
        factor = jnp.exp(tops - top)
        total = jnp.sum(stats_ref[:, 1, :] * factor, axis=0, keepdims=True)
        mean = jnp.sum(stats_ref[:, 2, :] * factor, axis=0, keepdims=True) / total
        inverse = 1.0 / total
        line = lax.broadcasted_iota(jnp.int32, (128, m), 0)
        column_ref[...] = jnp.where(line == 0, top, jnp.where(line == 1, inverse, mean)).T
        for i in range(2):
            vocab_start = (here ^ (8 * i)) * n
            curve_sum = jnp.zeros((1, n), F32)
            for j in range(8):
                at = slice(j * ROWS, (j + 1) * ROWS)
                place = row_place(here, j)
                values = column_ref[pl.ds(pl.multiple_of(place * ROWS, ROWS), ROWS), :]
                mine = pl.multiple_of(owner(here, j) * ROWS, ROWS)
                wanted = targets_ref[pl.ds(mine, ROWS), :]
                side = h_refs[i][at, :] * scale
                tangent = t_refs[i][at, :] + side
                probability = jnp.exp(l_refs[i][at, :] - values[:, 0:1]) * values[:, 1:2]
                curve = probability * (tangent - values[:, 2:3])
                column = lax.broadcasted_iota(jnp.int32, (ROWS, n), 1) + vocab_start
                gradient = probability - jnp.where(wanted == column, 1.0, 0.0)
                c_refs[i][at, :] = curve.astype(BF16)
                g_refs[i][at, :] = gradient.astype(BF16)
                curve_sum += jnp.sum(
                    curve * side + gradient * (p_refs[i][at, :] * scale), axis=0, keepdims=True
                )
            curve_ref[i : i + 1, :] = curve_sum

    vmem = pl.BlockSpec(memory_space=pltpu.VMEM)
    return pl.pallas_call(
        kernel,
        in_specs=[pl.BlockSpec(memory_space=pltpu.SMEM)] + [vmem] * 10,
        out_specs=[vmem] * 5,
        out_shape=[jax.ShapeDtypeStruct((m, n), BF16)] * 4 + [jax.ShapeDtypeStruct((2, n), F32)],
        scratch_shapes=[pltpu.VMEM((m, 128), F32)],
        compiler_params=pltpu.CompilerParams(vmem_limit_bytes=60 * MIB),
    )(me, *logits, *sides, *tangents, *probes, stats, targets)


def back(me, curves, gradients, tables, probes, root, turn, after=()):
    m, n = curves[0].shape
    width = 768
    part = width // 3
    steps = 4

    def kernel(me_ref, c0, c1, g0, g1, *refs):
        table_refs, outs, (held, sems) = refs[0:4], refs[4 + len(after) : 9 + len(after)], refs[-2:]
        step = pl.program_id(0)
        zl, y, c, zh, x = decode(me_ref[0])

        def copies(at):
            slot = 2 * (1 - turn) + (at >> 1)
            to_x = member(c, pair_of(c, x) ^ (slot >> 1), slot & 1)
            column = pl.multiple_of(((zh ^ (at & 1)) * 4 + to_x) * width, width)
            return [
                pltpu.make_async_copy(
                    table_refs[i].at[:, pl.ds(column, width)], held.at[at, i], sems.at[at, i]
                )
                for i in range(4)
            ]

        @pl.when(step == 0)
        def _():
            for copy in copies(0):
                copy.start()

        for copy in copies(step):
            copy.wait()

        @pl.when(step == 0)
        def _():
            for copy in copies(1):
                copy.start()

        @pl.when(step < steps - 2)
        def _():
            for copy in copies(step + 2):
                copy.start()

        total = jnp.dot(c0[...], held[step, 0], preferred_element_type=F32)
        total += jnp.dot(c1[...], held[step, 1], preferred_element_type=F32)
        total *= root
        total += jnp.dot(g0[...], held[step, 2], preferred_element_type=F32)
        total += jnp.dot(g1[...], held[step, 3], preferred_element_type=F32)

        def places(slot):
            place = row_place(me_ref[0], slot)
            zs = slot_of(c, 2 * zh + zl, 2 * (zh ^ (step & 1)) + (place >> 2))
            return zs, slot_of(c, y, place & 3), slice(slot * ROWS, (slot + 1) * ROWS)

        for slot in range(8):
            zs, ys, at = places(slot)
            outs[0][zs, ys, 0] = total[at, :part].astype(outs[0].dtype)
            if slot % 4 < 2:
                outs[2][zs, ys, 0] = total[at, part : 2 * part]
            else:
                outs[1][zs, ys - 2, 0] = total[at, part : 2 * part].astype(BF16)

        for half_rows in range(2):
            z_slot = places(4 * half_rows)[0]

            @pl.when(z_slot >= 2)
            def _():
                for slot in range(4 * half_rows, 4 * half_rows + 4):
                    zs, ys, at = places(slot)
                    outs[3][zs - 2, ys, 0] = total[at, 2 * part :].astype(BF16)

            @pl.when(z_slot < 2)
            def _():
                for slot in range(4 * half_rows, 4 * half_rows + 4):
                    zs, ys, at = places(slot)
                    outs[4][zs, ys, 0] = total[at, 2 * part :]

    shapes, specs = [], []
    for z, y, dtype in ((4, 4, F32 if turn else BF16), (4, 2, BF16), (4, 2, F32), (2, 4, BF16), (2, 4, F32)):
        shapes.append(jax.ShapeDtypeStruct((z, y, 2, ROWS, part), dtype))
        specs.append(pl.BlockSpec((z, y, 1, ROWS, part), lambda s, me: (0, 0, s >> 1, 0, 0)))
    return pl.pallas_call(
        kernel,
        grid_spec=pltpu.PrefetchScalarGridSpec(
            num_scalar_prefetch=1,
            grid=(steps,),
            in_specs=[pl.BlockSpec((m, n), lambda s, me: (0, 0))] * 4
            + [pl.BlockSpec(memory_space=pl.ANY)] * (4 + len(after)),
            out_specs=specs,
            scratch_shapes=[pltpu.VMEM((steps, 4, n, width), BF16), pltpu.SemaphoreType.DMA((steps, 4))],
        ),
        out_shape=shapes,
        compiler_params=pltpu.CompilerParams(vmem_limit_bytes=60 * MIB),
        cost_estimate=pl.CostEstimate(flops=MIB, bytes_accessed=MIB, transcendentals=0),
    )(me, *curves, *gradients, *tables, *probes, *after)


def body(hidden, targets, hidden_probe, table, table_probe):
    vocab_rows, width = table.shape
    token_count = targets.shape[0]
    vocab_total = vocab_rows * 128
    scale = 1.0 / math.sqrt(width)
    root = math.sqrt(width)
    me = lax.axis_index(AXES).astype(jnp.int32).reshape(1)

    own = hidden.reshape(1, 1, ROWS, width)
    got = swap(own, "y", 1)
    table_other = swap(table, "c")
    probe_other = swap(table_probe, "c")
    probe_rows = hidden_probe.reshape(token_count // ROWS, ROWS, width)
    t0 = probe_products(me, probe_rows, table)
    got = tie(got, t0)
    first = jnp.concatenate([own[..., :FIRST], got[..., :FIRST]], axis=1)
    second = jnp.concatenate([own[..., FIRST:], got[..., FIRST:]], axis=1)
    first_got, second_got = swap(first, "y", 0), swap(second, "z")
    p0 = probe_products(me, probe_rows, table_probe, after=(first, second))
    first = jnp.concatenate([first, tie(first_got, p0)], axis=1)
    second = jnp.concatenate([second, tie(second_got, p0)], axis=0)
    first_got, second_got = swap(first, "z"), swap(second, "y", 0)
    t1 = probe_products(me, probe_rows, table_other, after=(first, second))
    pieces = [a.reshape(4 * ROWS, -1) for a in (first, tie(first_got, t1), second, tie(second_got, t1))]
    p1 = probe_products(me, probe_rows, probe_other)
    l0, l1, h0, h1, stats = hidden_products(
        me, pieces, (table, table_other, table_probe, probe_other), (t0, t1), scale
    )
    stats = lax.all_to_all(
        stats,
        AXES,
        0,
        0,
        axis_index_groups=groups_of_core(),
        tiled=True,
    )
    c0, c1, g0, g1, curve = coefficients(
        me, (l0, l1), (h0, h1), (t0, t1), (p0, p1), stats, targets.reshape(token_count, 1), scale
    )
    curvature = (curve[0] + swap(curve[1], "c")) * (vocab_total / token_count)

    operands = (me, (c0, c1), (g0, g1), (table, table_other), (table_probe, probe_other), root)
    x_send, *early = back(*operands, 0)
    x_keep, *late = back(*operands, 1, after=(x_send,))

    def wide(a):
        return a.astype(F32)

    def halve(keep, axis):
        k = "zyx".index(axis)
        send = lax.slice_in_dim(keep, 2, 4, axis=k).astype(BF16)
        return lax.slice_in_dim(keep, 0, 2, axis=k) + wide(swap(send, axis))

    summed = [halve(halve(x_keep + wide(swap(x_send, "x")), "z"), "y")]
    for i, (axis, last) in enumerate((("y", "z"), ("z", "y"))):
        send = early[2 * i + 1] + wide(swap(early[2 * i], axis))
        keep = late[2 * i + 1] + wide(swap(late[2 * i], axis))
        summed.append(halve(keep + wide(swap(send.astype(BF16), "x")), last))
    total = jnp.concatenate(summed, axis=-1).astype(BF16).reshape(8, ROWS, width // 8)
    total = lax.all_to_all(total, AXES, 0, 0, axis_index_groups=groups_of_eight(), tiled=True)
    return jnp.sum(total.astype(F32), axis=0).astype(BF16), curvature


def solution(mesh):
    placed = (P("dp", None), P(), P(), P(("dp", "vocab"), None), P(("dp", "vocab"), None))
    return jax.shard_map(
        body,
        mesh=mesh,
        in_specs=placed,
        out_specs=(P("dp", "vocab"), P(("dp", "vocab"))),
        check_vma=False,
    )
```

```python
import math

import jax
import jax.numpy as jnp
from jax import lax
from jax.experimental import pallas as pl
from jax.experimental.pallas import tpu as pltpu
from jax.sharding import PartitionSpec as P

AXES = ("dp", "vocab")
F32 = jnp.float32
BF16 = jnp.bfloat16
FIRST = 3072
BLOCK = 1024
PROBE_BLOCK = 2048
ROWS = 48
MIB = 1 << 20
LIMIT = 60 * MIB
BACK_LIMIT = 40 * MIB
NT = (((1,), (1,)), ((), ()))


def decode(d):
    return (d >> 6) & 1, (d >> 4) & 3, (d >> 3) & 1, (d >> 2) & 1, d & 3


def encode(zl, y, c, zh, x):
    return (((zl * 4 + y) * 2 + c) * 2 + zh) * 4 + x


def pairs(axes, kind):
    out = []
    for d in range(128):
        zl, y, c, zh, x = decode(d)
        m = 1 if c == kind else 3
        for axis in axes:
            if axis == "x":
                x ^= m
            elif axis == "y":
                y ^= m
            elif axis == "z":
                z = (2 * zh + zl) ^ m
                zh, zl = z >> 1, z & 1
            else:
                c ^= 1
        out.append((d, encode(zl, y, c, zh, x)))
    return out


def swap(a, axis, kind=0):
    return lax.ppermute(a, AXES, pairs(axis, kind))


def pair_of(c, q):
    return jnp.where(c == 0, (q ^ (q >> 1)) & 1, q >> 1)


def bit_of(c, q):
    return jnp.where(c == 0, q >> 1, q & 1)


def member(c, pair, bit):
    return jnp.where(c == 0, pair * (1 + bit) + (1 - pair) * 3 * bit, 2 * pair + bit)


def slot_of(c, me, q):
    return 2 * (pair_of(c, me) ^ pair_of(c, q)) + bit_of(c, q)


def groups_of_eight():
    found = {}
    for d in range(128):
        zl, y, c, zh, x = decode(d)
        at = [2 * zh + zl, y, x]
        pair = [(q ^ (q >> 1)) & 1 if c == 0 else q >> 1 for q in at]
        bit = [q >> 1 if c == 0 else q & 1 for q in at]
        found.setdefault((c, *pair), {})[tuple(bit)] = d
    return [[g[b] for b in sorted(g)] for g in found.values()]


def groups_of_core():
    return [[d for d in range(128) if decode(d)[2] == c] for c in range(2)]


def row_place(me, slot):
    zl, y, c, _, _ = decode(me)
    zs, ys = slot // 4, slot % 4
    return (zl ^ zs) * 4 + (y ^ jnp.where(c == 0, (0, 3, 1, 2)[ys], (0, 1, 3, 2)[ys]))


def owner(me, slot):
    return row_place(me, slot) * 2 + ((me >> 3) & 1)


def tie(array, *after):
    def kernel(*refs):
        del refs

    return pl.pallas_call(
        kernel,
        in_specs=[pl.BlockSpec(memory_space=pl.ANY)] * (1 + len(after)),
        out_specs=pl.BlockSpec(memory_space=pl.ANY),
        out_shape=jax.ShapeDtypeStruct(array.shape, array.dtype),
        input_output_aliases={0: 0},
    )(array, *after)


def probe_products(me, rows, table, after=()):
    m, k = 8 * ROWS, rows.shape[-1]
    n = table.shape[0]

    def kernel(me_ref, *refs):
        row_refs, table_ref, out_ref = refs[:8], refs[8], refs[-1]
        block = jnp.concatenate([r[0] for r in row_refs], axis=0)

        @pl.when(pl.program_id(0) == 0)
        def _():
            out_ref[...] = jnp.zeros((m, n), F32)

        out_ref[...] += lax.dot_general(block, table_ref[...], NT, preferred_element_type=F32)

    return pl.pallas_call(
        kernel,
        grid_spec=pltpu.PrefetchScalarGridSpec(
            num_scalar_prefetch=1,
            grid=(k // PROBE_BLOCK,),
            in_specs=[
                pl.BlockSpec((1, ROWS, PROBE_BLOCK), lambda s, me, i=i: (owner(me[0], i), 0, s)) for i in range(8)
            ]
            + [pl.BlockSpec((n, PROBE_BLOCK), lambda s, me: (0, s))]
            + [pl.BlockSpec(memory_space=pl.ANY)] * len(after),
            out_specs=pl.BlockSpec((m, n), lambda s, me: (0, 0)),
        ),
        out_shape=jax.ShapeDtypeStruct((m, n), F32),
        compiler_params=pltpu.CompilerParams(vmem_limit_bytes=LIMIT),
        cost_estimate=pl.CostEstimate(flops=MIB, bytes_accessed=MIB, transcendentals=0),
    )(me, *([rows] * 8), table, *after)


def hidden_products(me, pieces, tables, tangents, scale):
    m = 8 * ROWS
    k = pieces[0].shape[1] + pieces[2].shape[1]
    n = tables[0].shape[0]
    steps = k // BLOCK
    split = FIRST // BLOCK
    pair = 2 * ROWS

    def kernel(me_ref, *refs):
        piece_refs, table_refs, tangent_refs = refs[0:4], refs[4:8], refs[8:10]
        outs, stats_ref = refs[10:14], refs[14]
        rows_ref, tables_ref, packed_ref, held_ref, sems, row_sems, table_sems = refs[15:22]
        step = pl.program_id(0)
        copies = [pltpu.make_async_copy(tangent_refs[i], held_ref.at[i], sems.at[i]) for i in range(2)]

        def row_copies(at):
            if at < split:
                parts = [(0, 0, 0, m // 2), (1, 0, m // 2, m // 2)]
                column = at * BLOCK
            else:
                parts = [(2 + i % 2, i // 2 * pair, i * pair, pair) for i in range(4)]
                column = (at - split) * BLOCK
            return [
                pltpu.make_async_copy(
                    piece_refs[p].at[pl.ds(source, length), pl.ds(column, BLOCK)],
                    rows_ref.at[at, pl.ds(target, length)],
                    row_sems.at[at, i],
                )
                for i, (p, source, target, length) in enumerate(parts)
            ]

        def table_copies(at):
            column = at * BLOCK
            return [
                pltpu.make_async_copy(
                    table_refs[i].at[:, pl.ds(column, BLOCK)], tables_ref.at[at, i], table_sems.at[at, i]
                )
                for i in range(4)
            ]

        @pl.when(step == 0)
        def _():
            for copy in row_copies(0) + table_copies(0):
                copy.start()
            for i in range(4):
                outs[i][...] = jnp.zeros((m, n), F32)

        for at in range(steps):

            @pl.when(step == at)
            def _():
                for copy in row_copies(at) + table_copies(at):
                    copy.wait()
                for then in ((1, 2) if at == 0 else (at + 2,)):
                    if then < steps:
                        for copy in row_copies(then) + table_copies(then):
                            copy.start()
                if at == 1:
                    for copy in copies:
                        copy.start()

        for i in range(4):
            outs[i][...] += lax.dot_general(
                rows_ref[step], tables_ref[step, i], NT, preferred_element_type=F32
            )

        @pl.when(step == steps - 1)
        def _():
            for copy in copies:
                copy.wait()
            lane = lax.broadcasted_iota(jnp.int32, (ROWS, 128), 1)
            for i in range(8):
                at = slice(i * ROWS, (i + 1) * ROWS)
                l0, l1 = outs[0][at, :], outs[1][at, :]
                t0 = held_ref[0, at, :] + outs[2][at, :] * scale
                t1 = held_ref[1, at, :] + outs[3][at, :] * scale
                top = jnp.maximum(jnp.max(l0, axis=1, keepdims=True), jnp.max(l1, axis=1, keepdims=True))
                e0 = jnp.exp(l0 - top)
                e1 = jnp.exp(l1 - top)
                total = jnp.sum(e0, axis=1, keepdims=True) + jnp.sum(e1, axis=1, keepdims=True)
                weighted = jnp.sum(e0 * t0, axis=1, keepdims=True) + jnp.sum(
                    e1 * t1, axis=1, keepdims=True
                )
                place = pl.multiple_of(row_place(me_ref[0], i) * ROWS, ROWS)
                packed_ref[pl.ds(place, ROWS), :] = jnp.where(
                    lane == 0, top, jnp.where(lane == 1, total, weighted)
                )
            stats_ref[...] = jnp.broadcast_to(packed_ref[...].T[0:3, :][None], (64, 3, m))

    return pl.pallas_call(
        kernel,
        grid_spec=pltpu.PrefetchScalarGridSpec(
            num_scalar_prefetch=1,
            grid=(steps,),
            in_specs=[pl.BlockSpec(memory_space=pl.ANY)] * 10,
            out_specs=[pl.BlockSpec((m, n), lambda s, me: (0, 0))] * 4
            + [pl.BlockSpec((64, 3, m), lambda s, me: (0, 0, 0))],
            scratch_shapes=[
                pltpu.VMEM((steps, m, BLOCK), BF16),
                pltpu.VMEM((steps, 4, n, BLOCK), BF16),
                pltpu.VMEM((m, 128), F32),
                pltpu.VMEM((2, m, n), F32),
                pltpu.SemaphoreType.DMA((2,)),
                pltpu.SemaphoreType.DMA((steps, 4)),
                pltpu.SemaphoreType.DMA((steps, 4)),
            ],
        ),
        out_shape=[jax.ShapeDtypeStruct((m, n), F32)] * 4 + [jax.ShapeDtypeStruct((64, 3, m), F32)],
        compiler_params=pltpu.CompilerParams(vmem_limit_bytes=LIMIT),
        cost_estimate=pl.CostEstimate(flops=MIB, bytes_accessed=MIB, transcendentals=0),
    )(me, *pieces, *tables, *tangents)


def coefficients(here, loads, arrays, stats_ref, targets_ref, c_refs, g_refs, curve_ref, column_ref, scale):
    m, n = c_refs[0].shape
    tops = stats_ref[:, 0, :]
    top = jnp.max(tops, axis=0, keepdims=True)
    factor = jnp.exp(tops - top)
    total = jnp.sum(stats_ref[:, 1, :] * factor, axis=0, keepdims=True)
    mean = jnp.sum(stats_ref[:, 2, :] * factor, axis=0, keepdims=True) / total
    inverse = 1.0 / total
    line = lax.broadcasted_iota(jnp.int32, (128, m), 0)
    column_ref[...] = jnp.where(line == 0, top, jnp.where(line == 1, inverse, mean)).T
    for i in range(2):
        for load in loads[i::2]:
            load.wait()
        vocab_start = (here ^ (8 * i)) * n
        curve_sum = jnp.zeros((1, n), F32)
        for j in range(8):
            at = slice(j * ROWS, (j + 1) * ROWS)
            place = row_place(here, j)
            values = column_ref[pl.ds(pl.multiple_of(place * ROWS, ROWS), ROWS), :]
            mine = pl.multiple_of(owner(here, j) * ROWS, ROWS)
            wanted = targets_ref[pl.ds(mine, ROWS), :]
            side = arrays[2 + i, at, :] * scale
            tangent = arrays[4 + i, at, :] + side
            probability = jnp.exp(arrays[i, at, :] - values[:, 0:1]) * values[:, 1:2]
            curve = probability * (tangent - values[:, 2:3])
            column = lax.broadcasted_iota(jnp.int32, (ROWS, n), 1) + vocab_start
            gradient = probability - jnp.where(wanted == column, 1.0, 0.0)
            c_refs[i][at, :] = curve.astype(BF16)
            g_refs[i][at, :] = gradient.astype(BF16)
            curve_sum += jnp.sum(
                curve * side + gradient * (arrays[6 + i, at, :] * scale), axis=0, keepdims=True
            )
        curve_ref[i : i + 1, :] = curve_sum


def back(me, tables, root, turn, factors=(), arrays=(), stats=None, targets=None, scale=1.0, after=()):
    m, n = 8 * ROWS, tables[0].shape[0]
    width = 768
    part = width // 3
    steps = 4
    made = turn == 0

    def kernel(me_ref, *refs):
        refs = list(refs)

        def take(length):
            taken = refs[:length]
            del refs[:length]
            return taken

        factor_refs = take(len(factors))
        table_refs = take(4)
        array_refs = take(len(arrays))
        if made:
            stats_ref, targets_ref = take(2)
        take(len(after))
        outs = take(5)
        if made:
            factor_refs = take(4)
            (curve_ref,) = take(1)
        held, sems = take(2)
        step = pl.program_id(0)
        here = me_ref[0]
        zl, y, c, zh, x = decode(here)
        c0, c1, g0, g1 = factor_refs

        def copies(at):
            slot = 2 * (1 - turn) + (at >> 1)
            to_x = member(c, pair_of(c, x) ^ (slot >> 1), slot & 1)
            column = pl.multiple_of(((zh ^ (at & 1)) * 4 + to_x) * width, width)
            return [
                pltpu.make_async_copy(
                    table_refs[i].at[:, pl.ds(column, width)], held.at[at, i], sems.at[at, i]
                )
                for i in range(4)
            ]

        @pl.when(step == 0)
        def _():
            if made:
                array_ref, array_sems, column_ref = refs
                loads = [
                    pltpu.make_async_copy(array_refs[i], array_ref.at[i], array_sems.at[i]) for i in range(8)
                ]
                for i in (0, 2, 4, 6, 1, 3, 5, 7):
                    loads[i].start()
            for copy in copies(0):
                copy.start()
            if made:
                for copy in copies(1):
                    copy.start()
                coefficients(
                    here,
                    loads,
                    array_ref,
                    stats_ref,
                    targets_ref,
                    factor_refs[:2],
                    factor_refs[2:],
                    curve_ref,
                    column_ref,
                    scale,
                )

        for copy in copies(step):
            copy.wait()

        if not made:

            @pl.when(step == 0)
            def _():
                for copy in copies(1):
                    copy.start()

        @pl.when(step < steps - 2)
        def _():
            for copy in copies(step + 2):
                copy.start()

        total = jnp.dot(c0[...], held[step, 0], preferred_element_type=F32)
        total += jnp.dot(c1[...], held[step, 1], preferred_element_type=F32)
        total *= root
        total += jnp.dot(g0[...], held[step, 2], preferred_element_type=F32)
        total += jnp.dot(g1[...], held[step, 3], preferred_element_type=F32)

        def places(slot):
            place = row_place(me_ref[0], slot)
            zs = slot_of(c, 2 * zh + zl, 2 * (zh ^ (step & 1)) + (place >> 2))
            return zs, slot_of(c, y, place & 3), slice(slot * ROWS, (slot + 1) * ROWS)

        for slot in range(8):
            zs, ys, at = places(slot)
            outs[0][zs, ys, 0] = total[at, :part].astype(outs[0].dtype)
            if slot % 4 < 2:
                outs[2][zs, ys, 0] = total[at, part : 2 * part]
            else:
                outs[1][zs, ys - 2, 0] = total[at, part : 2 * part].astype(BF16)

        for half_rows in range(2):
            z_slot = places(4 * half_rows)[0]

            @pl.when(z_slot >= 2)
            def _():
                for slot in range(4 * half_rows, 4 * half_rows + 4):
                    zs, ys, at = places(slot)
                    outs[3][zs - 2, ys, 0] = total[at, 2 * part :].astype(BF16)

            @pl.when(z_slot < 2)
            def _():
                for slot in range(4 * half_rows, 4 * half_rows + 4):
                    zs, ys, at = places(slot)
                    outs[4][zs, ys, 0] = total[at, 2 * part :]

    shapes, specs = [], []
    for z, y, dtype in ((4, 4, BF16 if made else F32), (4, 2, BF16), (4, 2, F32), (2, 4, BF16), (2, 4, F32)):
        shapes.append(jax.ShapeDtypeStruct((z, y, 2, ROWS, part), dtype))
        specs.append(pl.BlockSpec((z, y, 1, ROWS, part), lambda s, me: (0, 0, s >> 1, 0, 0)))
    whole = pl.BlockSpec((m, n), lambda s, me: (0, 0))
    anywhere = pl.BlockSpec(memory_space=pl.ANY)
    inputs = [me, *factors, *tables, *arrays]
    in_specs = (
        [whole] * len(factors)
        + [pl.BlockSpec(memory_space=pltpu.HBM)] * (4 + len(arrays))
    )
    scratch = [pltpu.VMEM((steps, 4, n, width), BF16), pltpu.SemaphoreType.DMA((steps, 4))]
    if made:
        inputs += [stats, targets]
        in_specs += [
            pl.BlockSpec(stats.shape, lambda s, me: (0, 0, 0)),
            pl.BlockSpec(targets.shape, lambda s, me: (0, 0)),
        ]
        shapes += [jax.ShapeDtypeStruct((m, n), BF16)] * 4 + [jax.ShapeDtypeStruct((2, n), F32)]
        specs += [whole] * 4 + [pl.BlockSpec((2, n), lambda s, me: (0, 0))]
        scratch += [pltpu.VMEM((8, m, n), F32), pltpu.SemaphoreType.DMA((8,)), pltpu.VMEM((m, 128), F32)]
    return pl.pallas_call(
        kernel,
        grid_spec=pltpu.PrefetchScalarGridSpec(
            num_scalar_prefetch=1,
            grid=(steps,),
            in_specs=in_specs + [anywhere] * len(after),
            out_specs=specs,
            scratch_shapes=scratch,
        ),
        out_shape=shapes,
        compiler_params=pltpu.CompilerParams(vmem_limit_bytes=BACK_LIMIT),
        cost_estimate=pl.CostEstimate(flops=MIB, bytes_accessed=MIB, transcendentals=0),
    )(*inputs, *after)


def body(hidden, targets, hidden_probe, table, table_probe):
    vocab_rows, width = table.shape
    token_count = targets.shape[0]
    vocab_total = vocab_rows * 128
    scale = 1.0 / math.sqrt(width)
    root = math.sqrt(width)
    me = lax.axis_index(AXES).astype(jnp.int32).reshape(1)

    own = hidden.reshape(1, 1, ROWS, width)
    got = swap(own, "y", 1)
    table_other = swap(table, "c")
    probe_other = swap(table_probe, "c")
    probe_rows = hidden_probe.reshape(token_count // ROWS, ROWS, width)
    t0 = probe_products(me, probe_rows, table)
    got = tie(got, t0)
    first = jnp.concatenate([own[..., :FIRST], got[..., :FIRST]], axis=1)
    second = jnp.concatenate([own[..., FIRST:], got[..., FIRST:]], axis=1)
    first_got, second_got = swap(first, "y", 0), swap(second, "z")
    p0 = probe_products(me, probe_rows, table_probe, after=(first, second))
    first = jnp.concatenate([first, tie(first_got, p0)], axis=1)
    second = jnp.concatenate([second, tie(second_got, p0)], axis=0)
    first_got, second_got = swap(first, "z"), swap(second, "y", 0)
    t1 = probe_products(me, probe_rows, table_other, after=(first, second))
    pieces = [a.reshape(4 * ROWS, -1) for a in (first, tie(first_got, t1), second, tie(second_got, t1))]
    p1 = probe_products(me, probe_rows, probe_other)
    l0, l1, h0, h1, stats = hidden_products(
        me, pieces, (table, table_other, table_probe, probe_other), (t0, t1), scale
    )
    stats = lax.all_to_all(
        stats,
        AXES,
        0,
        0,
        axis_index_groups=groups_of_core(),
        tiled=True,
    )
    tables = (table, table_other, table_probe, probe_other)
    x_send, *early = back(
        me,
        tables,
        root,
        0,
        arrays=(l0, l1, h0, h1, t0, t1, p0, p1),
        stats=stats,
        targets=targets.reshape(token_count, 1),
        scale=scale,
    )
    *early, curve = early
    x_keep, *late = back(me, tables, root, 1, factors=early[4:], after=(x_send,))
    curvature = (curve[0] + swap(curve[1], "c")) * (vocab_total / token_count)

    def wide(a):
        return a.astype(F32)

    def halve(keep, axis):
        k = "zyx".index(axis)
        send = lax.slice_in_dim(keep, 2, 4, axis=k).astype(BF16)
        return lax.slice_in_dim(keep, 0, 2, axis=k) + wide(swap(send, axis))

    x_got, y_got, z_got = swap(x_send, "x"), swap(early[0], "y"), swap(early[2], "z")
    summed = [halve(halve(x_keep + wide(x_got), "z"), "y")]
    for i, (axis, last, got) in enumerate((("y", "z", y_got), ("z", "y", z_got))):
        send = early[2 * i + 1] + wide(got)
        keep = late[2 * i + 1] + wide(swap(late[2 * i], axis))
        summed.append(halve(keep + wide(swap(send.astype(BF16), "x")), last))
    total = jnp.concatenate(summed, axis=-1).astype(BF16).reshape(8, ROWS, width // 8)
    total = lax.all_to_all(total, AXES, 0, 0, axis_index_groups=groups_of_eight(), tiled=True)
    return jnp.sum(total.astype(F32), axis=0).astype(BF16), curvature


def solution(mesh):
    placed = (P("dp", None), P(), P(), P(("dp", "vocab"), None), P(("dp", "vocab"), None))
    return jax.shard_map(
        body,
        mesh=mesh,
        in_specs=placed,
        out_specs=(P("dp", "vocab"), P(("dp", "vocab"))),
        check_vma=False,
    )
```

```python
import math

import jax
import jax.numpy as jnp
from jax import lax
from jax.experimental import pallas as pl
from jax.experimental.pallas import tpu as pltpu
from jax.sharding import PartitionSpec as P

AXES = ("dp", "vocab")
F32 = jnp.float32
BF16 = jnp.bfloat16
FIRST = 3072
BLOCK = 1024
PROBE_BLOCK = 2048
ROWS = 48
MIB = 1 << 20
LIMIT = 60 * MIB
BACK_LIMITS = (46 * MIB, 40 * MIB)
NT = (((1,), (1,)), ((), ()))


def decode(d):
    return (d >> 6) & 1, (d >> 4) & 3, (d >> 3) & 1, (d >> 2) & 1, d & 3


def encode(zl, y, c, zh, x):
    return (((zl * 4 + y) * 2 + c) * 2 + zh) * 4 + x


def pairs(axes, kind):
    out = []
    for d in range(128):
        zl, y, c, zh, x = decode(d)
        m = 1 if c == kind else 3
        for axis in axes:
            if axis == "x":
                x ^= m
            elif axis == "y":
                y ^= m
            elif axis == "z":
                z = (2 * zh + zl) ^ m
                zh, zl = z >> 1, z & 1
            else:
                c ^= 1
        out.append((d, encode(zl, y, c, zh, x)))
    return out


def swap(a, axis, kind=0):
    return lax.ppermute(a, AXES, pairs(axis, kind))


def pair_of(c, q):
    return jnp.where(c == 0, (q ^ (q >> 1)) & 1, q >> 1)


def bit_of(c, q):
    return jnp.where(c == 0, q >> 1, q & 1)


def member(c, pair, bit):
    return jnp.where(c == 0, pair * (1 + bit) + (1 - pair) * 3 * bit, 2 * pair + bit)


def slot_of(c, me, q):
    return 2 * (pair_of(c, me) ^ pair_of(c, q)) + bit_of(c, q)


def groups_of_eight():
    found = {}
    for d in range(128):
        zl, y, c, zh, x = decode(d)
        at = [2 * zh + zl, y, x]
        pair = [(q ^ (q >> 1)) & 1 if c == 0 else q >> 1 for q in at]
        bit = [q >> 1 if c == 0 else q & 1 for q in at]
        found.setdefault((c, *pair), {})[tuple(bit)] = d
    return [[g[b] for b in sorted(g)] for g in found.values()]


def groups_of_core():
    return [[d for d in range(128) if decode(d)[2] == c] for c in range(2)]


def row_place(me, slot):
    zl, y, c, _, _ = decode(me)
    zs, ys = slot // 4, slot % 4
    return (zl ^ zs) * 4 + (y ^ jnp.where(c == 0, (0, 3, 1, 2)[ys], (0, 1, 3, 2)[ys]))


def owner(me, slot):
    return row_place(me, slot) * 2 + ((me >> 3) & 1)


def tie(array, *after):
    def kernel(*refs):
        del refs

    return pl.pallas_call(
        kernel,
        in_specs=[pl.BlockSpec(memory_space=pl.ANY)] * (1 + len(after)),
        out_specs=pl.BlockSpec(memory_space=pl.ANY),
        out_shape=jax.ShapeDtypeStruct(array.shape, array.dtype),
        input_output_aliases={0: 0},
    )(array, *after)


def probe_products(me, rows, table, after=()):
    m, k = 8 * ROWS, rows.shape[-1]
    n = table.shape[0]

    def kernel(me_ref, *refs):
        row_refs, table_ref, out_ref = refs[:8], refs[8], refs[-1]
        block = jnp.concatenate([r[0] for r in row_refs], axis=0)

        @pl.when(pl.program_id(0) == 0)
        def _():
            out_ref[...] = jnp.zeros((m, n), F32)

        out_ref[...] += lax.dot_general(block, table_ref[...], NT, preferred_element_type=F32)

    return pl.pallas_call(
        kernel,
        grid_spec=pltpu.PrefetchScalarGridSpec(
            num_scalar_prefetch=1,
            grid=(k // PROBE_BLOCK,),
            in_specs=[
                pl.BlockSpec((1, ROWS, PROBE_BLOCK), lambda s, me, i=i: (owner(me[0], i), 0, s)) for i in range(8)
            ]
            + [pl.BlockSpec((n, PROBE_BLOCK), lambda s, me: (0, s))]
            + [pl.BlockSpec(memory_space=pl.ANY)] * len(after),
            out_specs=pl.BlockSpec((m, n), lambda s, me: (0, 0)),
        ),
        out_shape=jax.ShapeDtypeStruct((m, n), F32),
        compiler_params=pltpu.CompilerParams(vmem_limit_bytes=LIMIT),
        cost_estimate=pl.CostEstimate(flops=MIB, bytes_accessed=MIB, transcendentals=0),
    )(me, *([rows] * 8), table, *after)


def hidden_products(me, pieces, tables, tangents, scale):
    m = 8 * ROWS
    k = pieces[0].shape[1] + pieces[2].shape[1]
    n = tables[0].shape[0]
    steps = k // BLOCK
    split = FIRST // BLOCK
    pair = 2 * ROWS

    def kernel(me_ref, *refs):
        piece_refs, table_refs, tangent_refs = refs[0:4], refs[4:8], refs[8:10]
        outs, stats_ref = refs[10:14], refs[14]
        rows_ref, tables_ref, packed_ref, held_ref, sems, row_sems, table_sems = refs[15:22]
        step = pl.program_id(0)
        copies = [pltpu.make_async_copy(tangent_refs[i], held_ref.at[i], sems.at[i]) for i in range(2)]

        def row_copies(at):
            if at < split:
                parts = [(0, 0, 0, m // 2), (1, 0, m // 2, m // 2)]
                column = at * BLOCK
            else:
                parts = [(2 + i % 2, i // 2 * pair, i * pair, pair) for i in range(4)]
                column = (at - split) * BLOCK
            return [
                pltpu.make_async_copy(
                    piece_refs[p].at[pl.ds(source, length), pl.ds(column, BLOCK)],
                    rows_ref.at[at, pl.ds(target, length)],
                    row_sems.at[at, i],
                )
                for i, (p, source, target, length) in enumerate(parts)
            ]

        def table_copies(at):
            column = at * BLOCK
            return [
                pltpu.make_async_copy(
                    table_refs[i].at[:, pl.ds(column, BLOCK)], tables_ref.at[at, i], table_sems.at[at, i]
                )
                for i in range(4)
            ]

        @pl.when(step == 0)
        def _():
            for copy in row_copies(0) + table_copies(0):
                copy.start()
            for i in range(4):
                outs[i][...] = jnp.zeros((m, n), F32)

        for at in range(steps):

            @pl.when(step == at)
            def _():
                for copy in row_copies(at) + table_copies(at):
                    copy.wait()
                for then in ((1, 2) if at == 0 else (at + 2,)):
                    if then < steps:
                        for copy in row_copies(then) + table_copies(then):
                            copy.start()
                if at == 1:
                    for copy in copies:
                        copy.start()

        for i in range(4):
            outs[i][...] += lax.dot_general(
                rows_ref[step], tables_ref[step, i], NT, preferred_element_type=F32
            )

        @pl.when(step == steps - 1)
        def _():
            for copy in copies:
                copy.wait()
            lane = lax.broadcasted_iota(jnp.int32, (ROWS, 128), 1)
            for i in range(8):
                at = slice(i * ROWS, (i + 1) * ROWS)
                l0, l1 = outs[0][at, :], outs[1][at, :]
                t0 = held_ref[0, at, :] + outs[2][at, :] * scale
                t1 = held_ref[1, at, :] + outs[3][at, :] * scale
                top = jnp.maximum(jnp.max(l0, axis=1, keepdims=True), jnp.max(l1, axis=1, keepdims=True))
                e0 = jnp.exp(l0 - top)
                e1 = jnp.exp(l1 - top)
                total = jnp.sum(e0, axis=1, keepdims=True) + jnp.sum(e1, axis=1, keepdims=True)
                weighted = jnp.sum(e0 * t0, axis=1, keepdims=True) + jnp.sum(
                    e1 * t1, axis=1, keepdims=True
                )
                place = pl.multiple_of(row_place(me_ref[0], i) * ROWS, ROWS)
                packed_ref[pl.ds(place, ROWS), :] = jnp.where(
                    lane == 0, top, jnp.where(lane == 1, total, weighted)
                )
            stats_ref[...] = jnp.broadcast_to(packed_ref[...].T[0:3, :][None], (64, 3, m))

    return pl.pallas_call(
        kernel,
        grid_spec=pltpu.PrefetchScalarGridSpec(
            num_scalar_prefetch=1,
            grid=(steps,),
            in_specs=[pl.BlockSpec(memory_space=pl.ANY)] * 10,
            out_specs=[pl.BlockSpec((m, n), lambda s, me: (0, 0))] * 4
            + [pl.BlockSpec((64, 3, m), lambda s, me: (0, 0, 0))],
            scratch_shapes=[
                pltpu.VMEM((steps, m, BLOCK), BF16),
                pltpu.VMEM((steps, 4, n, BLOCK), BF16),
                pltpu.VMEM((m, 128), F32),
                pltpu.VMEM((2, m, n), F32),
                pltpu.SemaphoreType.DMA((2,)),
                pltpu.SemaphoreType.DMA((steps, 4)),
                pltpu.SemaphoreType.DMA((steps, 4)),
            ],
        ),
        out_shape=[jax.ShapeDtypeStruct((m, n), F32)] * 4 + [jax.ShapeDtypeStruct((64, 3, m), F32)],
        compiler_params=pltpu.CompilerParams(vmem_limit_bytes=LIMIT),
        cost_estimate=pl.CostEstimate(flops=MIB, bytes_accessed=MIB, transcendentals=0),
    )(me, *pieces, *tables, *tangents)


def coefficients(here, loads, arrays, stats_ref, targets_ref, c_refs, g_refs, curve_ref, column_ref, scale):
    m, n = c_refs[0].shape
    tops = stats_ref[:, 0, :]
    top = jnp.max(tops, axis=0, keepdims=True)
    factor = jnp.exp(tops - top)
    total = jnp.sum(stats_ref[:, 1, :] * factor, axis=0, keepdims=True)
    mean = jnp.sum(stats_ref[:, 2, :] * factor, axis=0, keepdims=True) / total
    inverse = 1.0 / total
    line = lax.broadcasted_iota(jnp.int32, (128, m), 0)
    column_ref[...] = jnp.where(line == 0, top, jnp.where(line == 1, inverse, mean)).T
    for i in range(2):
        for load in loads[i::2]:
            load.wait()
        vocab_start = (here ^ (8 * i)) * n
        curve_sum = jnp.zeros((1, n), F32)
        for j in range(8):
            at = slice(j * ROWS, (j + 1) * ROWS)
            place = row_place(here, j)
            values = column_ref[pl.ds(pl.multiple_of(place * ROWS, ROWS), ROWS), :]
            mine = pl.multiple_of(owner(here, j) * ROWS, ROWS)
            wanted = targets_ref[pl.ds(mine, ROWS), :]
            side = arrays[2 + i, at, :] * scale
            tangent = arrays[4 + i, at, :] + side
            probability = jnp.exp(arrays[i, at, :] - values[:, 0:1]) * values[:, 1:2]
            curve = probability * (tangent - values[:, 2:3])
            column = lax.broadcasted_iota(jnp.int32, (ROWS, n), 1) + vocab_start
            gradient = probability - jnp.where(wanted == column, 1.0, 0.0)
            c_refs[i][at, :] = curve.astype(BF16)
            g_refs[i][at, :] = gradient.astype(BF16)
            curve_sum += jnp.sum(
                curve * side + gradient * (arrays[6 + i, at, :] * scale), axis=0, keepdims=True
            )
        curve_ref[i : i + 1, :] = curve_sum


def back(me, tables, root, turn, factors=(), arrays=(), stats=None, targets=None, scale=1.0, after=()):
    m, n = 8 * ROWS, tables[0].shape[0]
    width = 768
    part = width // 3
    steps = 4
    made = turn == 0

    def kernel(me_ref, *refs):
        refs = list(refs)

        def take(length):
            taken = refs[:length]
            del refs[:length]
            return taken

        factor_refs = take(len(factors))
        table_refs = take(4)
        array_refs = take(len(arrays))
        if made:
            stats_ref, targets_ref = take(2)
        take(len(after))
        outs = take(5)
        if made:
            factor_refs = take(4)
            (curve_ref,) = take(1)
        held, sems = take(2)
        step = pl.program_id(0)
        here = me_ref[0]
        zl, y, c, zh, x = decode(here)
        c0, c1, g0, g1 = factor_refs

        def copies(at):
            slot = 2 * (1 - turn) + (at >> 1)
            to_x = member(c, pair_of(c, x) ^ (slot >> 1), slot & 1)
            column = pl.multiple_of(((zh ^ (at & 1)) * 4 + to_x) * width, width)
            return [
                pltpu.make_async_copy(
                    table_refs[i].at[:, pl.ds(column, width)], held.at[at, i], sems.at[at, i]
                )
                for i in range(4)
            ]

        @pl.when(step == 0)
        def _():
            if made:
                array_ref, array_sems, column_ref = refs
                loads = [
                    pltpu.make_async_copy(array_refs[i], array_ref.at[i], array_sems.at[i]) for i in range(8)
                ]
                for i in (0, 2, 4, 6, 1, 3, 5, 7):
                    loads[i].start()
            for copy in copies(0):
                copy.start()
            if made:
                for copy in copies(1):
                    copy.start()
                coefficients(
                    here,
                    loads,
                    array_ref,
                    stats_ref,
                    targets_ref,
                    factor_refs[:2],
                    factor_refs[2:],
                    curve_ref,
                    column_ref,
                    scale,
                )

        for copy in copies(step):
            copy.wait()

        if not made:

            @pl.when(step == 0)
            def _():
                for copy in copies(1):
                    copy.start()

        @pl.when(step < steps - 2)
        def _():
            for copy in copies(step + 2):
                copy.start()

        total = jnp.dot(c0[...], held[step, 0], preferred_element_type=F32)
        total += jnp.dot(c1[...], held[step, 1], preferred_element_type=F32)
        total *= root
        total += jnp.dot(g0[...], held[step, 2], preferred_element_type=F32)
        total += jnp.dot(g1[...], held[step, 3], preferred_element_type=F32)

        def places(slot):
            place = row_place(me_ref[0], slot)
            zs = slot_of(c, 2 * zh + zl, 2 * (zh ^ (step & 1)) + (place >> 2))
            return zs, slot_of(c, y, place & 3), slice(slot * ROWS, (slot + 1) * ROWS)

        for slot in range(8):
            zs, ys, at = places(slot)
            outs[0][zs, ys, 0] = total[at, :part].astype(outs[0].dtype)
            if slot % 4 < 2:
                outs[2][zs, ys, 0] = total[at, part : 2 * part]
            else:
                outs[1][zs, ys - 2, 0] = total[at, part : 2 * part].astype(BF16)

        for half_rows in range(2):
            z_slot = places(4 * half_rows)[0]

            @pl.when(z_slot >= 2)
            def _():
                for slot in range(4 * half_rows, 4 * half_rows + 4):
                    zs, ys, at = places(slot)
                    outs[3][zs - 2, ys, 0] = total[at, 2 * part :].astype(BF16)

            @pl.when(z_slot < 2)
            def _():
                for slot in range(4 * half_rows, 4 * half_rows + 4):
                    zs, ys, at = places(slot)
                    outs[4][zs, ys, 0] = total[at, 2 * part :]

    shapes, specs = [], []
    for z, y, dtype in ((4, 4, BF16 if made else F32), (4, 2, BF16), (4, 2, F32), (2, 4, BF16), (2, 4, F32)):
        shapes.append(jax.ShapeDtypeStruct((z, y, 2, ROWS, part), dtype))
        specs.append(pl.BlockSpec((z, y, 1, ROWS, part), lambda s, me: (0, 0, s >> 1, 0, 0)))
    whole = pl.BlockSpec((m, n), lambda s, me: (0, 0))
    anywhere = pl.BlockSpec(memory_space=pl.ANY)
    inputs = [me, *factors, *tables, *arrays]
    in_specs = (
        [whole] * len(factors)
        + [pl.BlockSpec(memory_space=pltpu.HBM)] * (4 + len(arrays))
    )
    scratch = [pltpu.VMEM((steps, 4, n, width), BF16), pltpu.SemaphoreType.DMA((steps, 4))]
    if made:
        inputs += [stats, targets]
        in_specs += [
            pl.BlockSpec(stats.shape, lambda s, me: (0, 0, 0)),
            pl.BlockSpec(targets.shape, lambda s, me: (0, 0)),
        ]
        shapes += [jax.ShapeDtypeStruct((m, n), BF16)] * 4 + [jax.ShapeDtypeStruct((2, n), F32)]
        specs += [whole] * 4 + [pl.BlockSpec((2, n), lambda s, me: (0, 0))]
        scratch += [pltpu.VMEM((8, m, n), F32), pltpu.SemaphoreType.DMA((8,)), pltpu.VMEM((m, 128), F32)]
    return pl.pallas_call(
        kernel,
        grid_spec=pltpu.PrefetchScalarGridSpec(
            num_scalar_prefetch=1,
            grid=(steps,),
            in_specs=in_specs + [anywhere] * len(after),
            out_specs=specs,
            scratch_shapes=scratch,
        ),
        out_shape=shapes,
        compiler_params=pltpu.CompilerParams(vmem_limit_bytes=BACK_LIMITS[turn]),
        cost_estimate=pl.CostEstimate(flops=MIB, bytes_accessed=MIB, transcendentals=0),
    )(*inputs, *after)


def body(hidden, targets, hidden_probe, table, table_probe):
    vocab_rows, width = table.shape
    token_count = targets.shape[0]
    vocab_total = vocab_rows * 128
    scale = 1.0 / math.sqrt(width)
    root = math.sqrt(width)
    me = lax.axis_index(AXES).astype(jnp.int32).reshape(1)

    own = hidden.reshape(1, 1, ROWS, width)
    got = swap(own, "y", 1)
    table_other = swap(table, "c")
    probe_other = swap(table_probe, "c")
    probe_rows = hidden_probe.reshape(token_count // ROWS, ROWS, width)
    t0 = probe_products(me, probe_rows, table)
    got = tie(got, t0)
    first = jnp.concatenate([own[..., :FIRST], got[..., :FIRST]], axis=1)
    second = jnp.concatenate([own[..., FIRST:], got[..., FIRST:]], axis=1)
    first_got, second_got = swap(first, "y", 0), swap(second, "z")
    p0 = probe_products(me, probe_rows, table_probe, after=(first, second))
    first = jnp.concatenate([first, tie(first_got, p0)], axis=1)
    second = jnp.concatenate([second, tie(second_got, p0)], axis=0)
    first_got, second_got = swap(first, "z"), swap(second, "y", 0)
    t1 = probe_products(me, probe_rows, table_other, after=(first, second))
    pieces = [a.reshape(4 * ROWS, -1) for a in (first, tie(first_got, t1), second, tie(second_got, t1))]
    p1 = probe_products(me, probe_rows, probe_other)
    l0, l1, h0, h1, stats = hidden_products(
        me, pieces, (table, table_other, table_probe, probe_other), (t0, t1), scale
    )
    stats = lax.all_to_all(
        stats,
        AXES,
        0,
        0,
        axis_index_groups=groups_of_core(),
        tiled=True,
    )
    tables = (table, table_other, table_probe, probe_other)
    x_send, *early = back(
        me,
        tables,
        root,
        0,
        arrays=(l0, l1, h0, h1, t0, t1, p0, p1),
        stats=stats,
        targets=targets.reshape(token_count, 1),
        scale=scale,
    )
    *early, curve = early
    x_keep, *late = back(me, tables, root, 1, factors=early[4:], after=(x_send,))
    curvature = (curve[0] + swap(curve[1], "c")) * (vocab_total / token_count)

    def wide(a):
        return a.astype(F32)

    def halve(keep, axis):
        k = "zyx".index(axis)
        send = lax.slice_in_dim(keep, 2, 4, axis=k).astype(BF16)
        return lax.slice_in_dim(keep, 0, 2, axis=k) + wide(swap(send, axis))

    x_got, y_got, z_got = swap(x_send, "x"), swap(early[0], "y"), swap(early[2], "z")
    summed = [halve(halve(x_keep + wide(x_got), "z"), "y")]
    for i, (axis, last, got) in enumerate((("y", "z", y_got), ("z", "y", z_got))):
        send = early[2 * i + 1] + wide(got)
        keep = late[2 * i + 1] + wide(swap(late[2 * i], axis))
        summed.append(halve(keep + wide(swap(send.astype(BF16), "x")), last))
    total = jnp.concatenate(summed, axis=-1).astype(BF16).reshape(8, ROWS, width // 8)
    total = lax.all_to_all(total, AXES, 0, 0, axis_index_groups=groups_of_eight(), tiled=True)
    return jnp.sum(total.astype(F32), axis=0).astype(BF16), curvature


def solution(mesh):
    placed = (P("dp", None), P(), P(), P(("dp", "vocab"), None), P(("dp", "vocab"), None))
    return jax.shard_map(
        body,
        mesh=mesh,
        in_specs=placed,
        out_specs=(P("dp", "vocab"), P(("dp", "vocab"))),
        check_vma=False,
    )
```

```python
import math

import jax
import jax.numpy as jnp
from jax import lax
from jax.experimental import pallas as pl
from jax.experimental.pallas import tpu as pltpu
from jax.sharding import PartitionSpec as P

AXES = ("dp", "vocab")
F32 = jnp.float32
BF16 = jnp.bfloat16
FIRST = 3072
BLOCK = 1024
PROBE_BLOCK = 2048
ROWS = 48
MIB = 1 << 20
LIMIT = 60 * MIB
BACK_LIMITS = (44 * MIB, 40 * MIB)
NT = (((1,), (1,)), ((), ()))


def decode(d):
    return (d >> 6) & 1, (d >> 4) & 3, (d >> 3) & 1, (d >> 2) & 1, d & 3


def encode(zl, y, c, zh, x):
    return (((zl * 4 + y) * 2 + c) * 2 + zh) * 4 + x


def pairs(axes, kind):
    out = []
    for d in range(128):
        zl, y, c, zh, x = decode(d)
        m = 1 if c == kind else 3
        for axis in axes:
            if axis == "x":
                x ^= m
            elif axis == "y":
                y ^= m
            elif axis == "z":
                z = (2 * zh + zl) ^ m
                zh, zl = z >> 1, z & 1
            else:
                c ^= 1
        out.append((d, encode(zl, y, c, zh, x)))
    return out


def swap(a, axis, kind=0):
    return lax.ppermute(a, AXES, pairs(axis, kind))


def pair_of(c, q):
    return jnp.where(c == 0, (q ^ (q >> 1)) & 1, q >> 1)


def bit_of(c, q):
    return jnp.where(c == 0, q >> 1, q & 1)


def member(c, pair, bit):
    return jnp.where(c == 0, pair * (1 + bit) + (1 - pair) * 3 * bit, 2 * pair + bit)


def slot_of(c, me, q):
    return 2 * (pair_of(c, me) ^ pair_of(c, q)) + bit_of(c, q)


def groups_of_eight():
    found = {}
    for d in range(128):
        zl, y, c, zh, x = decode(d)
        at = [2 * zh + zl, y, x]
        pair = [(q ^ (q >> 1)) & 1 if c == 0 else q >> 1 for q in at]
        bit = [q >> 1 if c == 0 else q & 1 for q in at]
        found.setdefault((c, *pair), {})[tuple(bit)] = d
    return [[g[b] for b in sorted(g)] for g in found.values()]


def groups_of_core():
    return [[d for d in range(128) if decode(d)[2] == c] for c in range(2)]


def row_place(me, slot):
    zl, y, c, _, _ = decode(me)
    zs, ys = slot // 4, slot % 4
    return (zl ^ zs) * 4 + (y ^ jnp.where(c == 0, (0, 3, 1, 2)[ys], (0, 1, 3, 2)[ys]))


def owner(me, slot):
    return row_place(me, slot) * 2 + ((me >> 3) & 1)


def tie(array, *after):
    def kernel(*refs):
        del refs

    return pl.pallas_call(
        kernel,
        in_specs=[pl.BlockSpec(memory_space=pl.ANY)] * (1 + len(after)),
        out_specs=pl.BlockSpec(memory_space=pl.ANY),
        out_shape=jax.ShapeDtypeStruct(array.shape, array.dtype),
        input_output_aliases={0: 0},
    )(array, *after)


def probe_products(me, rows, table, after=()):
    m, k = 8 * ROWS, rows.shape[-1]
    n = table.shape[0]

    def kernel(me_ref, *refs):
        row_refs, table_ref, out_ref = refs[:8], refs[8], refs[-1]
        block = jnp.concatenate([r[0] for r in row_refs], axis=0)

        @pl.when(pl.program_id(0) == 0)
        def _():
            out_ref[...] = jnp.zeros((m, n), F32)

        out_ref[...] += lax.dot_general(block, table_ref[...], NT, preferred_element_type=F32)

    return pl.pallas_call(
        kernel,
        grid_spec=pltpu.PrefetchScalarGridSpec(
            num_scalar_prefetch=1,
            grid=(k // PROBE_BLOCK,),
            in_specs=[
                pl.BlockSpec((1, ROWS, PROBE_BLOCK), lambda s, me, i=i: (owner(me[0], i), 0, s)) for i in range(8)
            ]
            + [pl.BlockSpec((n, PROBE_BLOCK), lambda s, me: (0, s))]
            + [pl.BlockSpec(memory_space=pl.ANY)] * len(after),
            out_specs=pl.BlockSpec((m, n), lambda s, me: (0, 0)),
        ),
        out_shape=jax.ShapeDtypeStruct((m, n), F32),
        compiler_params=pltpu.CompilerParams(vmem_limit_bytes=LIMIT),
        cost_estimate=pl.CostEstimate(flops=MIB, bytes_accessed=MIB, transcendentals=0),
    )(me, *([rows] * 8), table, *after)


def hidden_products(me, pieces, tables, tangents, scale):
    m = 8 * ROWS
    k = pieces[0].shape[1] + pieces[2].shape[1]
    n = tables[0].shape[0]
    steps = k // BLOCK
    split = FIRST // BLOCK
    pair = 2 * ROWS

    def kernel(me_ref, *refs):
        piece_refs, table_refs, tangent_refs = refs[0:4], refs[4:8], refs[8:10]
        outs, stats_ref = refs[10:14], refs[14]
        rows_ref, tables_ref, packed_ref, held_ref, sems, row_sems, table_sems = refs[15:22]
        step = pl.program_id(0)
        copies = [pltpu.make_async_copy(tangent_refs[i], held_ref.at[i], sems.at[i]) for i in range(2)]

        def row_copies(at):
            if at < split:
                parts = [(0, 0, 0, m // 2), (1, 0, m // 2, m // 2)]
                column = at * BLOCK
            else:
                parts = [(2 + i % 2, i // 2 * pair, i * pair, pair) for i in range(4)]
                column = (at - split) * BLOCK
            return [
                pltpu.make_async_copy(
                    piece_refs[p].at[pl.ds(source, length), pl.ds(column, BLOCK)],
                    rows_ref.at[at, pl.ds(target, length)],
                    row_sems.at[at, i],
                )
                for i, (p, source, target, length) in enumerate(parts)
            ]

        def table_copies(at):
            column = at * BLOCK
            return [
                pltpu.make_async_copy(
                    table_refs[i].at[:, pl.ds(column, BLOCK)], tables_ref.at[at, i], table_sems.at[at, i]
                )
                for i in range(4)
            ]

        @pl.when(step == 0)
        def _():
            for copy in row_copies(0) + table_copies(0):
                copy.start()
            for i in range(4):
                outs[i][...] = jnp.zeros((m, n), F32)

        for at in range(steps):

            @pl.when(step == at)
            def _():
                for copy in row_copies(at) + table_copies(at):
                    copy.wait()
                for then in ((1, 2) if at == 0 else (at + 2,)):
                    if then < steps:
                        for copy in row_copies(then) + table_copies(then):
                            copy.start()
                if at == 1:
                    for copy in copies:
                        copy.start()

        for i in range(4):
            outs[i][...] += lax.dot_general(
                rows_ref[step], tables_ref[step, i], NT, preferred_element_type=F32
            )

        @pl.when(step == steps - 1)
        def _():
            for copy in copies:
                copy.wait()
            lane = lax.broadcasted_iota(jnp.int32, (ROWS, 128), 1)
            for i in range(8):
                at = slice(i * ROWS, (i + 1) * ROWS)
                l0, l1 = outs[0][at, :], outs[1][at, :]
                t0 = held_ref[0, at, :] + outs[2][at, :] * scale
                t1 = held_ref[1, at, :] + outs[3][at, :] * scale
                top = jnp.maximum(jnp.max(l0, axis=1, keepdims=True), jnp.max(l1, axis=1, keepdims=True))
                e0 = jnp.exp(l0 - top)
                e1 = jnp.exp(l1 - top)
                total = jnp.sum(e0, axis=1, keepdims=True) + jnp.sum(e1, axis=1, keepdims=True)
                weighted = jnp.sum(e0 * t0, axis=1, keepdims=True) + jnp.sum(
                    e1 * t1, axis=1, keepdims=True
                )
                place = pl.multiple_of(row_place(me_ref[0], i) * ROWS, ROWS)
                packed_ref[pl.ds(place, ROWS), :] = jnp.where(
                    lane == 0, top, jnp.where(lane == 1, total, weighted)
                )
            stats_ref[...] = jnp.broadcast_to(packed_ref[...].T[0:3, :][None], (64, 3, m))

    return pl.pallas_call(
        kernel,
        grid_spec=pltpu.PrefetchScalarGridSpec(
            num_scalar_prefetch=1,
            grid=(steps,),
            in_specs=[pl.BlockSpec(memory_space=pl.ANY)] * 10,
            out_specs=[pl.BlockSpec((m, n), lambda s, me: (0, 0))] * 4
            + [pl.BlockSpec((64, 3, m), lambda s, me: (0, 0, 0))],
            scratch_shapes=[
                pltpu.VMEM((steps, m, BLOCK), BF16),
                pltpu.VMEM((steps, 4, n, BLOCK), BF16),
                pltpu.VMEM((m, 128), F32),
                pltpu.VMEM((2, m, n), F32),
                pltpu.SemaphoreType.DMA((2,)),
                pltpu.SemaphoreType.DMA((steps, 4)),
                pltpu.SemaphoreType.DMA((steps, 4)),
            ],
        ),
        out_shape=[jax.ShapeDtypeStruct((m, n), F32)] * 4 + [jax.ShapeDtypeStruct((64, 3, m), F32)],
        compiler_params=pltpu.CompilerParams(vmem_limit_bytes=LIMIT),
        cost_estimate=pl.CostEstimate(flops=MIB, bytes_accessed=MIB, transcendentals=0),
    )(me, *pieces, *tables, *tangents)


def coefficients(here, loads, arrays, stats_ref, targets_ref, c_refs, g_refs, curve_ref, column_ref, scale):
    m, n = c_refs[0].shape
    tops = stats_ref[:, 0, :]
    top = jnp.max(tops, axis=0, keepdims=True)
    factor = jnp.exp(tops - top)
    total = jnp.sum(stats_ref[:, 1, :] * factor, axis=0, keepdims=True)
    mean = jnp.sum(stats_ref[:, 2, :] * factor, axis=0, keepdims=True) / total
    inverse = 1.0 / total
    line = lax.broadcasted_iota(jnp.int32, (128, m), 0)
    column_ref[...] = jnp.where(line == 0, top, jnp.where(line == 1, inverse, mean)).T
    for i in range(2):
        for load in loads[i::2]:
            load.wait()
        vocab_start = (here ^ (8 * i)) * n
        curve_sum = jnp.zeros((1, n), F32)
        for j in range(8):
            at = slice(j * ROWS, (j + 1) * ROWS)
            place = row_place(here, j)
            values = column_ref[pl.ds(pl.multiple_of(place * ROWS, ROWS), ROWS), :]
            mine = pl.multiple_of(owner(here, j) * ROWS, ROWS)
            wanted = targets_ref[pl.ds(mine, ROWS), :]
            side = arrays[2 + i, at, :] * scale
            tangent = arrays[4 + i, at, :] + side
            probability = jnp.exp(arrays[i, at, :] - values[:, 0:1]) * values[:, 1:2]
            curve = probability * (tangent - values[:, 2:3])
            column = lax.broadcasted_iota(jnp.int32, (ROWS, n), 1) + vocab_start
            gradient = probability - jnp.where(wanted == column, 1.0, 0.0)
            c_refs[i][at, :] = curve.astype(BF16)
            g_refs[i][at, :] = gradient.astype(BF16)
            curve_sum += jnp.sum(
                curve * side + gradient * (arrays[6 + i, at, :] * scale), axis=0, keepdims=True
            )
        curve_ref[i : i + 1, :] = curve_sum


def back(me, tables, root, turn, factors=(), arrays=(), stats=None, targets=None, scale=1.0, after=()):
    m, n = 8 * ROWS, tables[0].shape[0]
    width = 768
    part = width // 3
    steps = 4
    made = turn == 0

    def kernel(me_ref, *refs):
        refs = list(refs)

        def take(length):
            taken = refs[:length]
            del refs[:length]
            return taken

        factor_refs = take(len(factors))
        table_refs = take(4)
        array_refs = take(len(arrays))
        if made:
            stats_ref, targets_ref = take(2)
        take(len(after))
        outs = take(5)
        if made:
            factor_refs = take(4)
            (curve_ref,) = take(1)
        held, sems = take(2)
        step = pl.program_id(0)
        here = me_ref[0]
        zl, y, c, zh, x = decode(here)
        c0, c1, g0, g1 = factor_refs

        def copies(at):
            slot = 2 * (1 - turn) + (at >> 1)
            to_x = member(c, pair_of(c, x) ^ (slot >> 1), slot & 1)
            column = pl.multiple_of(((zh ^ (at & 1)) * 4 + to_x) * width, width)
            return [
                pltpu.make_async_copy(
                    table_refs[i].at[:, pl.ds(column, width)], held.at[at, i], sems.at[at, i]
                )
                for i in range(4)
            ]

        @pl.when(step == 0)
        def _():
            if made:
                array_ref, array_sems, column_ref = refs
                loads = [
                    pltpu.make_async_copy(array_refs[i], array_ref.at[i], array_sems.at[i]) for i in range(8)
                ]
                for i in (0, 2, 4, 6, 1, 3, 5, 7):
                    loads[i].start()
            for copy in copies(0):
                copy.start()
            if made:
                for copy in copies(1):
                    copy.start()
                coefficients(
                    here,
                    loads,
                    array_ref,
                    stats_ref,
                    targets_ref,
                    factor_refs[:2],
                    factor_refs[2:],
                    curve_ref,
                    column_ref,
                    scale,
                )

        for copy in copies(step):
            copy.wait()

        if not made:

            @pl.when(step == 0)
            def _():
                for copy in copies(1):
                    copy.start()

        @pl.when(step < steps - 2)
        def _():
            for copy in copies(step + 2):
                copy.start()

        total = jnp.dot(c0[...], held[step, 0], preferred_element_type=F32)
        total += jnp.dot(c1[...], held[step, 1], preferred_element_type=F32)
        total *= root
        total += jnp.dot(g0[...], held[step, 2], preferred_element_type=F32)
        total += jnp.dot(g1[...], held[step, 3], preferred_element_type=F32)

        def places(slot):
            place = row_place(me_ref[0], slot)
            zs = slot_of(c, 2 * zh + zl, 2 * (zh ^ (step & 1)) + (place >> 2))
            return zs, slot_of(c, y, place & 3), slice(slot * ROWS, (slot + 1) * ROWS)

        for slot in range(8):
            zs, ys, at = places(slot)
            outs[0][zs, ys, 0] = total[at, :part].astype(outs[0].dtype)
            if slot % 4 < 2:
                outs[2][zs, ys, 0] = total[at, part : 2 * part]
            else:
                outs[1][zs, ys - 2, 0] = total[at, part : 2 * part].astype(BF16)

        for half_rows in range(2):
            z_slot = places(4 * half_rows)[0]

            @pl.when(z_slot >= 2)
            def _():
                for slot in range(4 * half_rows, 4 * half_rows + 4):
                    zs, ys, at = places(slot)
                    outs[3][zs - 2, ys, 0] = total[at, 2 * part :].astype(BF16)

            @pl.when(z_slot < 2)
            def _():
                for slot in range(4 * half_rows, 4 * half_rows + 4):
                    zs, ys, at = places(slot)
                    outs[4][zs, ys, 0] = total[at, 2 * part :]

    shapes, specs = [], []
    for z, y, dtype in ((4, 4, BF16 if made else F32), (4, 2, BF16), (4, 2, F32), (2, 4, BF16), (2, 4, F32)):
        shapes.append(jax.ShapeDtypeStruct((z, y, 2, ROWS, part), dtype))
        specs.append(pl.BlockSpec((z, y, 1, ROWS, part), lambda s, me: (0, 0, s >> 1, 0, 0)))
    whole = pl.BlockSpec((m, n), lambda s, me: (0, 0))
    anywhere = pl.BlockSpec(memory_space=pl.ANY)
    inputs = [me, *factors, *tables, *arrays]
    in_specs = (
        [whole] * len(factors)
        + [pl.BlockSpec(memory_space=pltpu.HBM)] * (4 + len(arrays))
    )
    scratch = [pltpu.VMEM((steps, 4, n, width), BF16), pltpu.SemaphoreType.DMA((steps, 4))]
    if made:
        inputs += [stats, targets]
        in_specs += [
            pl.BlockSpec(stats.shape, lambda s, me: (0, 0, 0)),
            pl.BlockSpec(targets.shape, lambda s, me: (0, 0)),
        ]
        shapes += [jax.ShapeDtypeStruct((m, n), BF16)] * 4 + [jax.ShapeDtypeStruct((2, n), F32)]
        specs += [whole] * 4 + [pl.BlockSpec((2, n), lambda s, me: (0, 0))]
        scratch += [pltpu.VMEM((8, m, n), F32), pltpu.SemaphoreType.DMA((8,)), pltpu.VMEM((m, 128), F32)]
    return pl.pallas_call(
        kernel,
        grid_spec=pltpu.PrefetchScalarGridSpec(
            num_scalar_prefetch=1,
            grid=(steps,),
            in_specs=in_specs + [anywhere] * len(after),
            out_specs=specs,
            scratch_shapes=scratch,
        ),
        out_shape=shapes,
        compiler_params=pltpu.CompilerParams(vmem_limit_bytes=BACK_LIMITS[turn]),
        cost_estimate=pl.CostEstimate(flops=MIB, bytes_accessed=MIB, transcendentals=0),
    )(*inputs, *after)


def body(hidden, targets, hidden_probe, table, table_probe):
    vocab_rows, width = table.shape
    token_count = targets.shape[0]
    vocab_total = vocab_rows * 128
    scale = 1.0 / math.sqrt(width)
    root = math.sqrt(width)
    me = lax.axis_index(AXES).astype(jnp.int32).reshape(1)

    own = hidden.reshape(1, 1, ROWS, width)
    got = swap(own, "y", 1)
    table_other = swap(table, "c")
    probe_other = swap(table_probe, "c")
    probe_rows = hidden_probe.reshape(token_count // ROWS, ROWS, width)
    t0 = probe_products(me, probe_rows, table)
    got = tie(got, t0)
    first = jnp.concatenate([own[..., :FIRST], got[..., :FIRST]], axis=1)
    second = jnp.concatenate([own[..., FIRST:], got[..., FIRST:]], axis=1)
    first_got, second_got = swap(first, "y", 0), swap(second, "z")
    p0 = probe_products(me, probe_rows, table_probe, after=(first, second))
    first = jnp.concatenate([first, tie(first_got, p0)], axis=1)
    second = jnp.concatenate([second, tie(second_got, p0)], axis=0)
    first_got, second_got = swap(first, "z"), swap(second, "y", 0)
    t1 = probe_products(me, probe_rows, table_other, after=(first, second))
    pieces = [a.reshape(4 * ROWS, -1) for a in (first, tie(first_got, t1), second, tie(second_got, t1))]
    p1 = probe_products(me, probe_rows, probe_other)
    l0, l1, h0, h1, stats = hidden_products(
        me, pieces, (table, table_other, table_probe, probe_other), (t0, t1), scale
    )
    stats = lax.all_to_all(
        stats,
        AXES,
        0,
        0,
        axis_index_groups=groups_of_core(),
        tiled=True,
    )
    tables = (table, table_other, table_probe, probe_other)
    x_send, *early = back(
        me,
        tables,
        root,
        0,
        arrays=(l0, l1, h0, h1, t0, t1, p0, p1),
        stats=stats,
        targets=targets.reshape(token_count, 1),
        scale=scale,
    )
    *early, curve = early
    x_keep, *late = back(me, tables, root, 1, factors=early[4:], after=(x_send,))
    curvature = (curve[0] + swap(curve[1], "c")) * (vocab_total / token_count)

    def wide(a):
        return a.astype(F32)

    def halve(keep, axis):
        k = "zyx".index(axis)
        send = lax.slice_in_dim(keep, 2, 4, axis=k).astype(BF16)
        return lax.slice_in_dim(keep, 0, 2, axis=k) + wide(swap(send, axis))

    x_got, y_got, z_got = swap(x_send, "x"), swap(early[0], "y"), swap(early[2], "z")
    summed = [halve(halve(x_keep + wide(x_got), "z"), "y")]
    for i, (axis, last, got) in enumerate((("y", "z", y_got), ("z", "y", z_got))):
        send = early[2 * i + 1] + wide(got)
        keep = late[2 * i + 1] + wide(swap(late[2 * i], axis))
        summed.append(halve(keep + wide(swap(send.astype(BF16), "x")), last))
    total = jnp.concatenate(summed, axis=-1).astype(BF16).reshape(8, ROWS, width // 8)
    total = lax.all_to_all(total, AXES, 0, 0, axis_index_groups=groups_of_eight(), tiled=True)
    return jnp.sum(total.astype(F32), axis=0).astype(BF16), curvature


def solution(mesh):
    placed = (P("dp", None), P(), P(), P(("dp", "vocab"), None), P(("dp", "vocab"), None))
    return jax.shard_map(
        body,
        mesh=mesh,
        in_specs=placed,
        out_specs=(P("dp", "vocab"), P(("dp", "vocab"))),
        check_vma=False,
    )
```
